32 devices in a mesh: section: 8 (over z, y), dp: 4 (over x, core).
Axes of the slice: x: 2, y: 2, z: 4, core: 2. Of those that a mesh axis runs over, the one named last changes fastest.
Arguments:
- enc_state: bfloat16 [8, 128, 4096], P('section', 'dp'), may hold values from -1000 to 1000
- final_gain: float32 [4096], replicated, may hold values from 0.5 to 1.5
- queries: bfloat16 [8, 512, 4096], P('section', 'dp'), may hold values from -60 to 60
- w_key: bfloat16 [8, 4096, 4096], P('section', None, 'dp'), may hold values from -0.09375 to 0.09375
- w_value: bfloat16 [8, 4096, 4096], P('section', None, 'dp'), may hold values from -0.09375 to 0.09375
- ctx_grad: bfloat16 [8, 512, 4096], P('section', 'dp'), may hold values from -6 to 6
- mem_len: int32 [4], P('dp'), may hold values from 8 to 32, as said below
Outputs:
- query_grad: bfloat16 [8, 512, 4096], P('section', 'dp')
- key_weight_grad: bfloat16 [8, 4096, 4096], P('section', None, 'dp')
- value_weight_grad: bfloat16 [8, 4096, 4096], P('section', None, 'dp')
- state_grad: bfloat16 [8, 128, 4096], P('section', 'dp')
- gain_grad: float32 [4096], replicated
The draws below stay inside these ranges and needn't reach their ends.
Inputs may be any that keep to these rules, and one draw needn't show every extreme that they name: Sequence b's memory holds mem_len[b] valid tokens from position 0; in every draw some sequence has all 32.
All inputs are finite; a program needn't handle non-finite values.
Results may differ from the reference program's by a relative error of at most 0.028.
The reference program's roundings to bfloat16 on the way count: a program that leaves them out, or rounds other values in their place, can miss the bound.
Values may be sent and summed in bfloat16 or wider, within the bound.
No kernel may reach another device: no remote copies, remote signals or barrier semaphores. Data moves between devices by JAX's collectives and lax.ppermute only.
A program may use at most 128 MiB of HBM per device.

```python
import math
import jax
import jax.numpy as jnp
from jax import lax

D = 4096
HEADS = 16
HEAD_DIM = 256
SRC = 32
TGT = 128
TGT_ROWS = 512
INNER = 4096
N_SECTION = 8
N_DP = 4


def draw_enc_state(key, part):
    split_keys = jax.random.split(jax.random.fold_in(key, 11), 2)
    noise = jax.random.truncated_normal(split_keys[0], -6.0, 6.0, (N_SECTION, N_DP * SRC, D), jnp.float32)
    row_scale = jnp.exp(jax.random.uniform(split_keys[1], (N_SECTION, N_DP * SRC, 1), jnp.float32, 0.0, math.log(10.0)))
    result = noise * row_scale
    return result.astype(jnp.bfloat16)


def draw_queries(key, part):
    split_keys = jax.random.split(jax.random.fold_in(key, 23), 1)
    shape = (N_SECTION, N_DP * TGT, HEADS * HEAD_DIM)
    result = jax.random.truncated_normal(split_keys[0], -6.0, 6.0, shape, jnp.float32)
    return result.astype(jnp.bfloat16)


def draw_mem_len(key, part):
    split_keys = jax.random.split(jax.random.fold_in(key, 37), 2)
    lengths = jax.random.randint(split_keys[0], (N_DP,), SRC // 4, SRC + 1)
    filled = jax.random.randint(split_keys[1], (), 0, N_DP)
    return jnp.where(jnp.arange(N_DP) == filled, SRC, lengths).astype(jnp.int32)


def levels(rng, dims, cuts, smallest, top_value):
    level, own = 1.0, jax.random.fold_in(rng, 6)
    for position, parts in cuts:
        heights = jnp.exp(jax.random.uniform(jax.random.fold_in(own, position), (parts,), jnp.float32, smallest / len(cuts), top_value / len(cuts)))
        level = level * jnp.repeat(heights, dims[position] // parts).reshape([-1 if axis == position else 1 for axis in range(len(dims))])
    return level


def bell_draw(key, extent, spread, most, cuts=(), held_as=jnp.bfloat16):
    values = spread * jax.random.normal(key, extent, jnp.float32)
    if cuts:
        values = values * levels(key, extent, cuts, -0.22, 0.18)
    return jnp.clip(values, -most, most).astype(held_as)


def setup_inputs(seed: int = 0) -> dict:
    streams_of = jax.random.split(jax.random.key(seed), 8)
    enc_state = draw_enc_state(jax.random.fold_in(streams_of[7], 71), 0)
    final_gain = jnp.clip(1.0 + 0.1 * jax.random.normal(streams_of[1], (D,), jnp.float32), 0.5, 1.5)
    queries = draw_queries(jax.random.fold_in(streams_of[7], 71), 0)
    w_key = bell_draw(streams_of[3], (N_SECTION, D, INNER), D ** -0.5, 0.09375, ((0, 8), (2, 4)))
    w_value = bell_draw(streams_of[4], (N_SECTION, D, INNER), D ** -0.5, 0.09375, ((0, 8), (2, 4)))
    ctx_grad = bell_draw(streams_of[5], (N_SECTION, TGT_ROWS, INNER), 1.0, 6.0, ((0, 8), (1, 4)))
    mem_len = draw_mem_len(jax.random.fold_in(streams_of[7], 71), 0)
    return {"enc_state": enc_state, "final_gain": final_gain, "queries": queries, "w_key": w_key, "w_value": w_value, "ctx_grad": ctx_grad, "mem_len": mem_len}


epsilon = 1e-06

def rounded(values):
    return lax.optimization_barrier(values.astype(jnp.bfloat16)).astype(jnp.float32)

def reference(enc_state, final_gain, queries, w_key, w_value, ctx_grad, mem_len):
    last_encoder = N_SECTION // 2 - 1
    first_decoder = N_SECTION // 2
    width = HEADS * HEAD_DIM
    enc_rows = enc_state[last_encoder].astype(jnp.float32)
    inverse = lax.rsqrt(lax.optimization_barrier(jnp.mean(enc_rows * enc_rows, axis=1, keepdims=True)) + epsilon)
    normed = enc_rows * inverse
    memory = (normed * final_gain).astype(jnp.bfloat16)
    key_valid = jnp.arange(SRC, dtype=jnp.int32)[None, :] < mem_len.astype(jnp.int32)[:, None]
    score_scale = HEAD_DIM ** (-0.5)

    def one_section(carry, inputs):
        section_queries, section_wk, section_wv, section_grad = inputs
        key_rows = jnp.dot(memory, section_wk, preferred_element_type=jnp.float32).astype(jnp.bfloat16)
        value_rows = jnp.dot(memory, section_wv, preferred_element_type=jnp.float32).astype(jnp.bfloat16)
        query_heads = section_queries.astype(jnp.float32).reshape(N_DP, TGT, HEADS, HEAD_DIM)
        grad_heads = section_grad.astype(jnp.float32).reshape(N_DP, TGT, HEADS, HEAD_DIM)
        key_heads = key_rows.astype(jnp.float32).reshape(N_DP, SRC, HEADS, HEAD_DIM)
        value_heads = value_rows.astype(jnp.float32).reshape(N_DP, SRC, HEADS, HEAD_DIM)
        scores = jnp.einsum('btha,buha->bhut', query_heads, key_heads) * score_scale
        scores = jnp.where(key_valid[:, None, :, None], scores, -1e+30)
        row_max = lax.optimization_barrier(jnp.max(scores, axis=2, keepdims=True))
        exponent = jnp.exp(scores - row_max)
        probs = exponent / lax.optimization_barrier(jnp.sum(exponent, axis=2, keepdims=True))
        grad_probs = jnp.einsum('btha,buha->bhut', grad_heads, value_heads)
        row_delta = lax.optimization_barrier(jnp.sum(probs * grad_probs, axis=2, keepdims=True))
        grad_scores = rounded(probs * (grad_probs - row_delta) * score_scale)
        query_grad = jnp.einsum('bhut,buha->btha', grad_scores, key_heads).reshape(N_DP * TGT, width).astype(jnp.bfloat16)
        key_grad = jnp.einsum('bhut,btha->buha', grad_scores, query_heads).reshape(N_DP * SRC, width).astype(jnp.bfloat16)
        value_grad = jnp.einsum('bhut,btha->buha', rounded(probs), grad_heads).reshape(N_DP * SRC, width).astype(jnp.bfloat16)
        key_weight = lax.dot_general(memory, key_grad, (((0,), (0,)), ((), ())), preferred_element_type=jnp.float32).astype(jnp.bfloat16)
        value_weight = lax.dot_general(memory, value_grad, (((0,), (0,)), ((), ())), preferred_element_type=jnp.float32).astype(jnp.bfloat16)
        carry = carry + lax.dot_general(key_grad, section_wk, (((1,), (1,)), ((), ())), preferred_element_type=jnp.float32)
        carry = carry + lax.dot_general(value_grad, section_wv, (((1,), (1,)), ((), ())), preferred_element_type=jnp.float32)
        return (carry, (query_grad, key_weight, value_weight))
    start_grad = jnp.zeros((N_DP * SRC, D), jnp.float32)
    memory_grad, stacked = lax.scan(one_section, start_grad, (queries[first_decoder:], w_key[first_decoder:], w_value[first_decoder:], ctx_grad[first_decoder:]))
    query_grads, key_weights, value_weights = stacked
    query_grad = jnp.concatenate([jnp.zeros((first_decoder, N_DP * TGT, width), jnp.bfloat16), query_grads], axis=0)
    key_weight_grad = jnp.concatenate([jnp.zeros((first_decoder, D, width), jnp.bfloat16), key_weights], axis=0)
    value_weight_grad = jnp.concatenate([jnp.zeros((first_decoder, D, width), jnp.bfloat16), value_weights], axis=0)
    gain_grad = lax.optimization_barrier(jnp.sum(memory_grad * normed, axis=0))
    scaled_grad = memory_grad * final_gain
    last_grad = (inverse * (scaled_grad - normed * lax.optimization_barrier(jnp.mean(scaled_grad * normed, axis=1, keepdims=True)))).astype(jnp.bfloat16)
    state_grad = jnp.concatenate([jnp.zeros((last_encoder, N_DP * SRC, D), jnp.bfloat16), last_grad[None], jnp.zeros((N_SECTION - first_decoder, N_DP * SRC, D), jnp.bfloat16)], axis=0)
    return (query_grad, key_weight_grad, value_weight_grad, state_grad, gain_grad)
```

```python
import jax
import jax.numpy as jnp
from jax import lax
from jax.sharding import PartitionSpec as P

HEAD_DIM = 256
epsilon = 1e-06
BOTH = ("section", "dp")


def section_rounds(sections):
    half = sections // 2
    source = half - 1
    first = min(half + 1, sections - 1)
    held = {source, first}
    rounds = [[(source, first)]]
    if source > 0 and half + 2 < sections:
        rounds[0].append((source, source - 1))
        held.add(source - 1)
    stage = []
    for a, b in ((first, first + 2), (source - 1, source + 3), (first, first - 1)):
        if a in held and half <= b < sections and b not in held:
            stage.append((a, b))
            held.add(b)
    if stage:
        rounds.append(stage)
    while not held.issuperset(range(half, sections)):
        have = [s for s in sorted(held) if s >= half]
        stage = []
        for a in have:
            b = a + len(have)
            if b < sections and b not in held:
                stage.append((a, b))
                held.add(b)
        rounds.append(stage)
    return rounds


def split_pairs(stage):
    groups = []
    for a, b in stage:
        for group in groups:
            if all(a != c and b != e for c, e in group):
                group.append((a, b))
                break
        else:
            groups.append([(a, b)])
    return groups


def on_device(enc_state, final_gain, queries, w_key, w_value, ctx_grad, mem_len):
    sections = lax.axis_size("section")
    replicas = lax.axis_size("dp")
    section_index = lax.axis_index("section")
    replica = lax.axis_index("dp")
    half = sections // 2
    last_encoder = half - 1
    bits = replicas.bit_length() - 1
    assert replicas == 1 << bits and sections & (sections - 1) == 0
    src_len, width = enc_state.shape[1:]
    tgt_len = queries.shape[1]
    local_width = w_key.shape[2]
    heads_here = local_width // HEAD_DIM
    score_scale = HEAD_DIM ** (-0.5)
    is_last = section_index == last_encoder

    def over_dp(block, k, first=0):
        pairs = [
            (s * replicas + d, s * replicas + (d ^ k))
            for s in range(first, sections)
            for d in range(replicas)
        ]
        return lax.ppermute(block, BOTH, pairs)

    def over_section(block, pairs):
        pairs = [(a * replicas + d, b * replicas + d) for a, b in pairs for d in range(replicas)]
        return lax.ppermute(block, BOTH, pairs)

    order = [0]
    for bit in reversed(range(bits)):
        order = order + [k ^ (1 << bit) for k in order]

    enc_rows = enc_state[0].astype(jnp.float32)
    inverse = lax.rsqrt(jnp.mean(enc_rows * enc_rows, axis=1, keepdims=True) + epsilon)
    normed = enc_rows * inverse
    memory = (normed * final_gain).astype(jnp.bfloat16)
    rounds = section_rounds(sections)
    holding = memory
    arrived = []
    for number, stage in enumerate(rounds):
        came = []
        for group in split_pairs(stage):
            block = over_section(holding, group)
            came.append(block)
            if all(b >= half for _, b in group):
                arrived.append(block)
        passed = came if number == 0 else arrived
        holding = sum(passed[1:], passed[0])
    all_memory = sum(arrived[1:], arrived[0])
    for bit in reversed(range(bits)):
        all_memory = jnp.concatenate([all_memory, over_dp(all_memory, 1 << bit, half)], axis=0)

    lengths = [mem_len] + [over_dp(mem_len, k) for k in range(1, replicas)]
    all_len = jnp.concatenate([lengths[k] for k in order])

    both = jnp.stack([queries[0], ctx_grad[0]])
    shares = []
    for k in range(replicas):
        start = (replica ^ k) * local_width
        share = lax.dynamic_slice(both, (0, 0, start), (2, tgt_len, local_width))
        shares.append(share if k == 0 else over_dp(share, k, half))
    gathered = jnp.stack([shares[k] for k in order]).reshape(
        replicas, 2, tgt_len, heads_here, HEAD_DIM
    )
    query_rows, grad_rows = gathered[:, 0], gathered[:, 1]

    def project(weight):
        rows = jnp.dot(all_memory, weight[0], preferred_element_type=jnp.float32)
        return rows.astype(jnp.bfloat16).reshape(replicas, src_len, heads_here, HEAD_DIM)

    key_rows, value_rows = project(w_key), project(w_value)
    key_valid = jnp.arange(src_len, dtype=jnp.int32)[None, :] < all_len[:, None]
    scores = (
        jnp.einsum("btha,buha->bhut", query_rows, key_rows, preferred_element_type=jnp.float32)
        * score_scale
    )
    scores = jnp.where(key_valid[:, None, :, None], scores, -1e30)
    row_max = jnp.max(scores, axis=2, keepdims=True)
    exponent = jnp.exp(scores - row_max)
    probs = exponent / jnp.sum(exponent, axis=2, keepdims=True)
    probs_low = probs.astype(jnp.bfloat16)
    grad_probs = jnp.einsum(
        "btha,buha->bhut", grad_rows, value_rows, preferred_element_type=jnp.float32
    )
    row_delta = jnp.sum(probs * grad_probs, axis=2, keepdims=True)
    grad_scores = (probs * (grad_probs - row_delta) * score_scale).astype(jnp.bfloat16)
    key_grad = (
        jnp.einsum("bhut,btha->buha", grad_scores, query_rows, preferred_element_type=jnp.float32)
        .astype(jnp.bfloat16)
        .reshape(replicas * src_len, local_width)
    )
    value_grad = (
        jnp.einsum("bhut,btha->buha", probs_low, grad_rows, preferred_element_type=jnp.float32)
        .astype(jnp.bfloat16)
        .reshape(replicas * src_len, local_width)
    )

    across = (((1,), (1,)), ((), ()))
    part = (
        lax.dot_general(key_grad, w_key[0], across, preferred_element_type=jnp.float32)
        + lax.dot_general(value_grad, w_value[0], across, preferred_element_type=jnp.float32)
    ).astype(jnp.bfloat16)
    gain_part = jnp.sum(part.astype(jnp.float32) * all_memory.astype(jnp.float32), axis=0)
    total = part.astype(jnp.float32)
    for bit in range(bits):
        keep = total.shape[0] // 2
        sent = total[keep:].astype(jnp.bfloat16)
        total = total[:keep] + over_dp(sent, 1 << bit, half).astype(jnp.float32)
    is_decoder = section_index >= half
    total = jnp.where(is_decoder, total, 0.0)
    for stage in reversed(rounds):
        sent = total.astype(jnp.bfloat16)
        for group in split_pairs(stage):
            total = total + over_section(sent, [(b, a) for a, b in group]).astype(jnp.float32)
    memory_grad = total
    scaled_grad = memory_grad * final_gain
    last_grad = inverse * (
        scaled_grad - normed * jnp.mean(scaled_grad * normed, axis=1, keepdims=True)
    )
    state_grad = jnp.where(is_last, last_grad, 0.0).astype(jnp.bfloat16)[None]

    query_grad_heads = (
        jnp.einsum("bhut,buha->btha", grad_scores, key_rows, preferred_element_type=jnp.float32)
        .astype(jnp.bfloat16)
        .reshape(replicas, tgt_len, local_width)
    )
    query_grad = jnp.zeros((tgt_len, replicas * local_width), jnp.bfloat16)
    for place, k in enumerate(order):
        share = query_grad_heads[place]
        share = share if k == 0 else over_dp(share, k, half)
        query_grad = lax.dynamic_update_slice(query_grad, share, (0, (replica ^ k) * local_width))

    down = (((0,), (0,)), ((), ()))
    key_weight_grad = lax.dot_general(
        all_memory, key_grad, down, preferred_element_type=jnp.float32
    ).astype(jnp.bfloat16)
    value_weight_grad = lax.dot_general(
        all_memory, value_grad, down, preferred_element_type=jnp.float32
    ).astype(jnp.bfloat16)

    gain_grad = gain_part / final_gain
    for bit in range(bits):
        gain_grad = gain_grad + over_dp(gain_grad, 1 << bit)
    step = 1
    while step < sections:
        pairs = [(s, s ^ step) for s in range(sections)]
        gain_grad = gain_grad + over_section(gain_grad, pairs)
        step *= 2
    return (
        query_grad[None],
        key_weight_grad[None],
        value_weight_grad[None],
        state_grad,
        gain_grad,
    )


def solution(mesh):
    placed = (
        P("section", "dp", None),
        P(),
        P("section", "dp", None),
        P("section", None, "dp"),
        P("section", None, "dp"),
        P("section", "dp", None),
        P("dp"),
    )
    return jax.shard_map(
        on_device,
        mesh=mesh,
        in_specs=placed,
        out_specs=(
            P("section", "dp", None),
            P("section", None, "dp"),
            P("section", None, "dp"),
            P("section", "dp", None),
            P(),
        ),
        check_vma=False,
    )
```

```python
import jax
import jax.numpy as jnp
from jax import lax
from jax.experimental import pallas as pl
from jax.experimental.pallas import tpu as pltpu
from jax.sharding import PartitionSpec as P

HEAD_DIM = 256
epsilon = 1e-06
BOTH = ("section", "dp")
LANES = 128


def section_rounds(sections):
    half = sections // 2
    source = half - 1
    first = min(half + 1, sections - 1)
    held = {source, first}
    rounds = [[(source, first)]]
    if source > 0 and half + 2 < sections:
        rounds[0].append((source, source - 1))
        held.add(source - 1)
    stage = []
    for a, b in ((first, first + 2), (source - 1, source + 3), (first, first - 1)):
        if a in held and half <= b < sections and b not in held:
            stage.append((a, b))
            held.add(b)
    if stage:
        rounds.append(stage)
    while not held.issuperset(range(half, sections)):
        have = [s for s in sorted(held) if s >= half]
        stage = []
        for a in have:
            b = a + len(have)
            if b < sections and b not in held:
                stage.append((a, b))
                held.add(b)
        rounds.append(stage)
    return rounds


def split_pairs(stage):
    groups = []
    for a, b in stage:
        for group in groups:
            if all(a != c and b != e for c, e in group):
                group.append((a, b))
                break
        else:
            groups.append([(a, b)])
    return groups


def call(kernel, out_shape, flops=0, moved=0, vmem=16, **options):
    return pl.pallas_call(
        kernel,
        out_shape=out_shape,
        compiler_params=pltpu.CompilerParams(vmem_limit_bytes=vmem << 20),
        cost_estimate=pl.CostEstimate(flops=flops, bytes_accessed=moved, transcendentals=0),
        **options,
    )


def shape(dims, dtype=jnp.bfloat16):
    return jax.ShapeDtypeStruct(dims, dtype)


def dot(a, b, dims=((1,), (0,))):
    return lax.dot_general(a, b, (dims, ((), ())), preferred_element_type=jnp.float32)


SMEM = pl.BlockSpec(memory_space=pltpu.SMEM)
VMEM = pl.BlockSpec(memory_space=pltpu.VMEM)
ANY = pl.BlockSpec(memory_space=pl.ANY)
TOKEN = shape((8, LANES), jnp.float32)


def mark(token_ref):
    token_ref[...] = jnp.zeros_like(token_ref)


def encode(mem_len, enc_state, gain):
    rows, width = enc_state.shape[1:]
    assert rows <= 256

    def kernel(len_ref, enc_ref, gain_ref, out_ref):
        state = enc_ref[0].astype(jnp.float32)
        inverse = lax.rsqrt(jnp.mean(state * state, axis=1, keepdims=True) + epsilon)
        out_ref[:, :width] = (state * inverse * gain_ref[...]).astype(jnp.bfloat16)
        length = jnp.full((rows, LANES), len_ref[0].astype(jnp.float32))
        out_ref[:, width:] = length.astype(jnp.bfloat16)

    return call(
        kernel,
        shape((rows, width + LANES)),
        moved=4 * rows * width,
        in_specs=[SMEM, VMEM, VMEM],
        out_specs=VMEM,
    )(mem_len, enc_state, gain)


def split_heads(scalars, queries, ctx_grad, replicas, tokens):
    rows, width = queries.shape[1:]
    piece = width // replicas
    sizes = []
    while replicas > 1 << len(sizes):
        sizes.append(replicas >> (len(sizes) + 1))
    starts = [*sizes, 0]
    sizes.append(1)

    def kernel(scalar_ref, query_ref, grad_ref, *refs):
        *out_refs, token_ref, sems = refs[len(tokens) :]
        copies = []
        for start, size, out_ref in zip(starts, sizes, out_refs, strict=True):
            for k in range(start, start + size):
                columns = pl.ds(pl.multiple_of((scalar_ref[0] ^ k) * piece, piece), piece)
                for i, ref in enumerate((query_ref, grad_ref)):
                    place = out_ref.at[k - start, i]
                    copy = pltpu.make_async_copy(ref.at[0, :, columns], place, sems.at[k, i])
                    copy.start()
                    copies.append(copy)
        mark(token_ref)
        for copy in copies:
            copy.wait()

    *shares, token = call(
        kernel,
        [shape((size, 2, rows, piece)) for size in sizes] + [TOKEN],
        moved=8 * rows * width,
        in_specs=[SMEM] + [ANY] * (2 + len(tokens)),
        out_specs=[ANY] * len(sizes) + [VMEM],
        scratch_shapes=[pltpu.SemaphoreType.DMA((replicas, 2))],
    )(scalars, queries, ctx_grad, *tokens)
    return shares, token


def add_blocks(blocks, tokens=()):
    def kernel(*refs):
        total = refs[0][...]
        for ref in refs[1 : len(blocks)]:
            total = total + ref[...]
        refs[-1][...] = total

    return call(
        kernel,
        shape(blocks[0].shape),
        moved=8 * blocks[0].size,
        in_specs=[VMEM] * len(blocks) + [ANY] * len(tokens),
        out_specs=VMEM,
    )(*blocks, *tokens)


def join_heads(shares):
    replicas, rows, piece = shares.shape

    def kernel(share_ref, out_ref, sems):
        copies = []
        for k in range(replicas):
            columns = pl.ds(k * piece, piece)
            copy = pltpu.make_async_copy(share_ref.at[k], out_ref.at[0, :, columns], sems.at[k])
            copy.start()
            copies.append(copy)
        for copy in copies:
            copy.wait()

    return call(
        kernel,
        shape((1, rows, replicas * piece)),
        moved=4 * rows * replicas * piece,
        in_specs=[ANY],
        out_specs=ANY,
        scratch_shapes=[pltpu.SemaphoreType.DMA((replicas,))],
    )(shares)


def hold_weights(w_key, w_value, tokens):
    steps = 4
    step = w_key.shape[1] // steps

    def kernel(wk_ref, wv_ref, *refs):
        *out_refs, token_ref, sems = refs[len(tokens) :]
        copies = []
        for i in range(steps):
            rows = pl.ds(i * step, step)
            for j, (ref, out_ref) in enumerate(zip((wk_ref, wv_ref), out_refs, strict=True)):
                copy = pltpu.make_async_copy(ref.at[0, rows], out_ref.at[0, rows], sems.at[i, j])
                copy.start()
                copies.append(copy)
        mark(token_ref)
        for copy in copies:
            copy.wait()

    *held, token = call(
        kernel,
        [shape(w_key.shape)] * 2 + [TOKEN],
        flops=1 << 34,
        moved=4 * w_key.size,
        vmem=36,
        in_specs=[ANY] * (2 + len(tokens)),
        out_specs=[ANY, ANY, VMEM],
        scratch_shapes=[pltpu.SemaphoreType.DMA((steps, 2))],
    )(w_key, w_value, *tokens)
    return held, token


def follow(block, tokens):
    def kernel(*refs):
        del refs

    return call(
        kernel,
        shape(block.shape, block.dtype),
        in_specs=[ANY] * (1 + len(tokens)),
        out_specs=ANY,
        input_output_aliases={0: 0},
    )(block, *tokens)


def attend(scalars, pieces, w_key, w_value, shares, order):
    count = len(pieces)
    rows = pieces[0].shape[0]
    depth, width = w_key.shape[1:]
    targets = shares[0].shape[2]
    scale = HEAD_DIM ** (-0.5)
    heads = width // HEAD_DIM

    def kernel(scalar_ref, *refs):
        wk_ref, wv_ref, *share_refs = refs[count : 2 * count + 2]
        dk_ref, dv_ref, dq_ref = refs[2 * count + 2 : 2 * count + 5]
        key_ref, value_ref, score_ref, grad_ref, low_ref = refs[2 * count + 5 :]
        memory = jnp.concatenate([ref[:, :depth] for ref in refs[:count]], axis=0)
        key_ref[...] = dot(memory, wk_ref[0]).astype(jnp.bfloat16)
        value_ref[...] = dot(memory, wv_ref[0]).astype(jnp.bfloat16)
        blocks = []
        for h in range(heads):
            for p, k in enumerate(order):
                head, own = slice(h * HEAD_DIM, (h + 1) * HEAD_DIM), slice(p * rows, (p + 1) * rows)
                blocks.append((head, own, scalar_ref[0] ^ k, share_refs[p]))
        for i, (head, own, _, share_ref) in enumerate(blocks):
            query, grad = share_ref[0, 0, :, head], share_ref[0, 1, :, head]
            score_ref[i] = dot(key_ref[own, head], query, ((1,), (1,)))
            grad_ref[i] = dot(value_ref[own, head], grad, ((1,), (1,)))
        token = lax.broadcasted_iota(jnp.int32, (rows, targets), 0).astype(jnp.float32)
        lengths = [ref[0:1, depth : depth + 1].astype(jnp.float32) for ref in refs[:count]]
        valid = jnp.stack([token < length for length in lengths])
        for h in range(heads):
            here = slice(h * count, (h + 1) * count)
            scores = jnp.where(valid, score_ref[here] * scale, -1e30)
            exponent = jnp.exp(scores - jnp.max(scores, axis=1, keepdims=True))
            probs = exponent / jnp.sum(exponent, axis=1, keepdims=True)
            grad_probs = grad_ref[here]
            delta = jnp.sum(probs * grad_probs, axis=1, keepdims=True)
            low_ref[0, here] = (probs * (grad_probs - delta) * scale).astype(jnp.bfloat16)
            low_ref[1, here] = probs.astype(jnp.bfloat16)
        is_decoder = scalar_ref[1].astype(jnp.float32)
        for i, (head, own, place, share_ref) in enumerate(blocks):
            query, grad = share_ref[0, 0, :, head], share_ref[0, 1, :, head]
            dk_ref[own, head] = dot(low_ref[0, i], query).astype(jnp.bfloat16)
            dv_ref[own, head] = (dot(low_ref[1, i], grad) * is_decoder).astype(jnp.bfloat16)
            dq = dot(low_ref[0, i], key_ref[own, head], ((0,), (0,)))
            dq_ref[place, :, head] = dq.astype(jnp.bfloat16)

    scores = (heads * count, rows, targets)
    return call(
        kernel,
        [shape((count * rows, width))] * 2 + [shape((count, targets, width))],
        flops=4 * count * rows * depth * width + 10 * count * rows * targets * width,
        moved=4 * depth * width + 8 * count * targets * width,
        in_specs=[SMEM] + [VMEM] * (2 * count + 2),
        out_specs=[VMEM] * 3,
        scratch_shapes=[
            *[pltpu.VMEM((count * rows, width), jnp.bfloat16)] * 2,
            *[pltpu.VMEM(scores, jnp.float32)] * 2,
            pltpu.VMEM((2, *scores), jnp.bfloat16),
        ],
    )(scalars, *pieces, w_key, w_value, *shares)


def memory_part(pieces, w_key, w_value, dk, dv, gain):
    count = len(pieces)
    rows = pieces[0].shape[0]
    depth, width = w_key.shape[1:]
    tile = 512
    steps = depth // tile
    keep = count * rows // 2

    def kernel(*refs):
        dk_ref, dv_ref, wk_ref, wv_ref, gain_ref, keep_ref, sent_ref, out_ref = refs[count:]
        for f in range(steps):
            here = slice(f * tile, (f + 1) * tile)
            part = dot(wk_ref[0, here, :], dk_ref[...], ((1,), (1,)))
            part = (part + dot(wv_ref[0, here, :], dv_ref[...], ((1,), (1,)))).T
            keep_ref[:, here] = part[:keep]
            sent_ref[:, here] = part[keep:].astype(jnp.bfloat16)
            total = jnp.zeros((1, tile), jnp.float32)
            for p in range(count):
                memory = refs[p][:, here].astype(jnp.float32)
                total += jnp.sum(part[p * rows : (p + 1) * rows] * memory, axis=0, keepdims=True)
            total = total / gain_ref[:, here]
            for i in range(tile // LANES):
                place = (f * tile) // LANES + i
                out_ref[place : place + 1, :] = total[:, i * LANES : (i + 1) * LANES]
        put_gain(out_ref[...], sent_ref)

    return call(
        kernel,
        [
            shape((keep, depth), jnp.float32),
            shape((keep, depth + 2 * LANES)),
            shape((depth // LANES, LANES), jnp.float32),
        ],
        flops=4 * count * rows * depth * width,
        moved=4 * depth * width,
        in_specs=[VMEM] * (count + 5),
        out_specs=[VMEM] * 3,
    )(*pieces, dk, dv, w_key, w_value, gain)


def put_gain(gain, sent_ref):
    rows = gain.shape[0]
    depth = sent_ref.shape[1] - 2 * LANES
    assert sent_ref.shape[0] >= rows
    high = gain.astype(jnp.bfloat16)
    if sent_ref.shape[0] > rows:
        sent_ref[rows:, depth:] = jnp.zeros((sent_ref.shape[0] - rows, 2 * LANES), jnp.bfloat16)
    sent_ref[:rows, depth : depth + LANES] = high
    sent_ref[:rows, depth + LANES :] = (gain - high.astype(jnp.float32)).astype(jnp.bfloat16)


def add_share(kept, came, gain, last, tokens=()):
    rows, depth = kept.shape
    half = rows if last else rows // 2

    def kernel(kept_ref, came_ref, gain_ref, *refs):
        keep_ref, sent_ref, out_ref, token_ref = refs[len(tokens) :]
        out = gain_ref.shape[0]
        came_gain = came_ref[:out, depth:].astype(jnp.float32)
        total_gain = gain_ref[...] + (came_gain[:, :LANES] + came_gain[:, LANES:])
        out_ref[...] = total_gain
        keep_ref[...] = kept_ref[:half] + came_ref[:half, :depth].astype(jnp.float32)
        if last:
            sent_ref[...] = keep_ref[...].astype(jnp.bfloat16)
        else:
            other = kept_ref[half:] + came_ref[half:, :depth].astype(jnp.float32)
            sent_ref[:, :depth] = other.astype(jnp.bfloat16)
            put_gain(total_gain, sent_ref)
        mark(token_ref)

    return call(
        kernel,
        [
            shape((half, depth), jnp.float32),
            shape((half, depth + (0 if last else 2 * LANES))),
            shape(gain.shape, jnp.float32),
            TOKEN,
        ],
        moved=10 * rows * depth,
        in_specs=[VMEM] * 3 + [ANY] * len(tokens),
        out_specs=[VMEM] * 4,
    )(kept, came, gain, *tokens)


def add_sections(kept, came, tokens=()):
    count = len(came)

    def kernel(kept_ref, *refs):
        keep_ref, sent_ref, token_ref = refs[count + len(tokens) :]
        total = kept_ref[...]
        for ref in refs[:count]:
            total = total + ref[...].astype(jnp.float32)
        keep_ref[...] = total
        sent_ref[...] = total.astype(jnp.bfloat16)
        mark(token_ref)

    return call(
        kernel,
        [shape(kept.shape, jnp.float32), shape(kept.shape), TOKEN],
        moved=12 * kept.size,
        in_specs=[VMEM] * (1 + count) + [ANY] * len(tokens),
        out_specs=[VMEM] * 3,
    )(kept, *came, *tokens)


def weight_grads(pieces, width, part, parts, dk, dv, before, tokens=()):
    count = len(pieces)
    rows = pieces[0].shape[0]
    columns = dk.shape[1]
    tile = 1024
    steps = width // (parts * tile)

    def kernel(*refs):
        memory = jnp.concatenate([ref[...] for ref in refs[:count]], axis=0)
        dk_ref, dv_ref = refs[count : count + 2]
        key_ref, value_ref, token_ref = refs[-3:]
        key_ref[0] = dot(memory, dk_ref[...], ((0,), (0,))).astype(jnp.bfloat16)
        value_ref[0] = dot(memory, dv_ref[...], ((0,), (0,))).astype(jnp.bfloat16)
        mark(token_ref)

    piece = pl.BlockSpec((rows, tile), lambda f: (0, part * steps + f))
    whole = pl.BlockSpec((count * rows, columns), lambda f: (0, 0))
    out = pl.BlockSpec((1, tile, columns), lambda f: (0, part * steps + f, 0))
    first = count + 2 + len(tokens)
    *grads, token = call(
        kernel,
        [shape((1, width, columns))] * 2 + [TOKEN],
        flops=4 * count * rows * width * columns // parts,
        moved=4 * width * columns // parts,
        vmem=24,
        grid=(steps,),
        in_specs=[piece] * count + [whole] * 2 + [ANY] * (len(tokens) + len(before)),
        out_specs=[out] * 2 + [pl.BlockSpec(TOKEN.shape, lambda f: (0, 0))],
        input_output_aliases={first + i: i for i in range(len(before))},
    )(*pieces, dk, dv, *tokens, *before)
    return grads, token


def finish(flag, enc_state, gain, terms):
    rows, width = enc_state.shape[1:]

    def kernel(flag_ref, enc_ref, gain_ref, *refs):
        state = enc_ref[0].astype(jnp.float32)
        inverse = lax.rsqrt(jnp.mean(state * state, axis=1, keepdims=True) + epsilon)
        normed = state * inverse
        own = [ref[...].astype(jnp.float32) for ref in refs[:-1]]
        scaled = sum(own[1:], own[0]) * gain_ref[...]
        mean = jnp.mean(scaled * normed, axis=1, keepdims=True)
        grad = inverse * (scaled - normed * mean)
        refs[-1][0] = jnp.where(flag_ref[0] > 0, grad, 0.0).astype(jnp.bfloat16)

    return call(
        kernel,
        shape((1, rows, width)),
        moved=8 * rows * width,
        in_specs=[SMEM] + [VMEM] * (2 + len(terms)),
        out_specs=VMEM,
    )(flag, enc_state, gain, *terms)


def on_device(enc_state, final_gain, queries, w_key, w_value, ctx_grad, mem_len):
    sections = lax.axis_size("section")
    replicas = lax.axis_size("dp")
    section_index = lax.axis_index("section")
    half = sections // 2
    bits = replicas.bit_length() - 1
    assert replicas == 1 << bits and half & (half - 1) == 0 and half > 1 and bits > 1
    is_decoder = (section_index >= half).astype(jnp.int32)
    is_last = (section_index == half - 1).astype(jnp.int32)[None]
    scalars = jnp.stack([lax.axis_index("dp").astype(jnp.int32), is_decoder])
    gain = final_gain[None]

    def over_dp(block, k):
        pairs = [
            (s * replicas + d, s * replicas + (d ^ k))
            for s in range(half, sections)
            for d in range(replicas)
        ]
        return lax.ppermute(block, BOTH, pairs)

    def over_section(block, pairs):
        pairs = [(a * replicas + d, b * replicas + d) for a, b in pairs for d in range(replicas)]
        return lax.ppermute(block, BOTH, pairs)

    order = [0]
    for bit in reversed(range(bits)):
        order = order + [k ^ (1 << bit) for k in order]
    rounds = section_rounds(sections)

    memory = encode(mem_len, enc_state, gain)
    shares, split = split_heads(scalars, queries, ctx_grad, replicas, [memory])
    came = {}
    for bit, share in zip(reversed(range(bits)), shares, strict=False):
        size = 1 << bit
        passed = {k ^ size: over_dp(block[size : 2 * size], size) for k, block in came.items()}
        came = came | passed | {size: over_dp(share, size)}
    came[0] = shares[-1]
    shares = [came[k] for k in order]
    came = [over_section(memory, group) for group in split_pairs(rounds[0])]
    arrived = [came[0]]
    holding = add_blocks(came, [split])
    weights, held = hold_weights(w_key, w_value, [holding])
    for stage in rounds[1:]:
        arrived += [over_section(holding, group) for group in split_pairs(stage)]
        holding = add_blocks(arrived, [held])
    pieces = {0: holding}
    for bit in reversed(range(bits)):
        pieces |= {k ^ (1 << bit): over_dp(pieces[k], 1 << bit) for k in list(pieces)}
    pieces = [pieces[k] for k in order]
    dk, dv, dq = attend(scalars, pieces, *weights, shares, order)

    kept, sent, gain_part = memory_part(pieces, *weights, dk, dv, gain)
    width = enc_state.shape[2]
    decoders = range(half, sections)
    parts = 4
    grads, token = [], None
    for bit in range(bits):
        last = bit == bits - 1
        came = over_dp(sent, 1 << bit)
        tokens = []
        if last:
            for part in range(parts - 1):
                grads, token = weight_grads(pieces, width, part, parts, dk, dv, grads, [token])
            tokens = [token]
        kept, sent, gain_part, token = add_share(kept, came, gain_part, last, tokens)
    dq = follow(dq, [token])
    grads, token = weight_grads(pieces, width, parts - 1, parts, dk, dv, grads, [token])
    key_weight_grad, value_weight_grad = grads
    step = 1
    while step < half // 2:
        gain_part = gain_part + over_section(gain_part, [(s, s ^ step) for s in decoders])
        step *= 2
    tokens = [token, gain_part]
    for number, stage in reversed(list(enumerate(rounds))):
        came = [over_section(sent, [(b, a) for a, b in group]) for group in split_pairs(stage)]
        if number:
            kept, sent, _ = add_sections(kept, came, tokens)
            tokens = []
    state_grad = finish(is_last, enc_state, gain, came)
    gain_part = (
        gain_part
        + over_section(gain_part, [(s, s ^ step) for s in decoders])
        + over_section(gain_part, [(s, s - half) for s in decoders])
        + over_section(gain_part, [(s, (s ^ step) - half) for s in decoders])
    )

    query_grad = join_heads(lax.all_to_all(dq, "dp", split_axis=0, concat_axis=0, tiled=True))

    gain_grad = gain_part.reshape(width)
    return (query_grad, key_weight_grad, value_weight_grad, state_grad, gain_grad)


def solution(mesh):
    placed = (
        P("section", "dp", None),
        P(),
        P("section", "dp", None),
        P("section", None, "dp"),
        P("section", None, "dp"),
        P("section", "dp", None),
        P("dp"),
    )
    return jax.shard_map(
        on_device,
        mesh=mesh,
        in_specs=placed,
        out_specs=(
            P("section", "dp", None),
            P("section", None, "dp"),
            P("section", None, "dp"),
            P("section", "dp", None),
            P(),
        ),
        check_vma=False,
    )
```

```python
import jax
import jax.numpy as jnp
from jax import lax
from jax.experimental import pallas as pl
from jax.experimental.pallas import tpu as pltpu
from jax.sharding import PartitionSpec as P

HEAD_DIM = 256
epsilon = 1e-06
BOTH = ("section", "dp")
LANES = 128
TILE = 1024
VMEM_BEGIN = 54
COST_HOLD = 1 << 32
COST_SUM = 1 << 32


def section_rounds(sections):
    half = sections // 2
    source = half - 1
    first = min(half + 1, sections - 1)
    held = {source, first}
    rounds = [[(source, first)]]
    if source > 0 and half + 2 < sections:
        rounds[0].append((source, source - 1))
        held.add(source - 1)
    stage = []
    for a, b in ((first, first + 2), (source - 1, source + 3), (first, first - 1)):
        if a in held and half <= b < sections and b not in held:
            stage.append((a, b))
            held.add(b)
    if stage:
        rounds.append(stage)
    while not held.issuperset(range(half, sections)):
        have = [s for s in sorted(held) if s >= half]
        stage = []
        for a in have:
            b = a + len(have)
            if b < sections and b not in held:
                stage.append((a, b))
                held.add(b)
        rounds.append(stage)
    return rounds


def split_pairs(stage):
    groups = []
    for a, b in stage:
        for group in groups:
            if all(a != c and b != e for c, e in group):
                group.append((a, b))
                break
        else:
            groups.append([(a, b)])
    return groups


def call(kernel, out_shape, flops=0, moved=0, vmem=16, **options):
    return pl.pallas_call(
        kernel,
        out_shape=out_shape,
        compiler_params=pltpu.CompilerParams(vmem_limit_bytes=vmem << 20),
        cost_estimate=pl.CostEstimate(flops=flops, bytes_accessed=moved, transcendentals=0),
        **options,
    )


def shape(dims, dtype=jnp.bfloat16):
    return jax.ShapeDtypeStruct(dims, dtype)


def dot(a, b, dims=((1,), (0,))):
    return lax.dot_general(a, b, (dims, ((), ())), preferred_element_type=jnp.float32)


SMEM = pl.BlockSpec(memory_space=pltpu.SMEM)
VMEM = pl.BlockSpec(memory_space=pltpu.VMEM)
ANY = pl.BlockSpec(memory_space=pl.ANY)
TOKEN = shape((8, LANES), jnp.float32)


def mark(token_ref):
    token_ref[...] = jnp.zeros_like(token_ref)


def begin(enc_state, gain, queries, ctx_grad, replicas):
    rows, width = enc_state.shape[1:]
    targets = queries.shape[1]
    piece = width // replicas
    half = replicas // 2

    def kernel(enc_ref, gain_ref, query_ref, grad_ref, out_ref, far_ref, held, held_gain, sems, far_sems):
        first = [
            pltpu.make_async_copy(enc_ref.at[0], held, sems.at[0]),
            pltpu.make_async_copy(gain_ref, held_gain, sems.at[1]),
        ]
        for copy in first:
            copy.start()
        index = lax.axis_index("dp")
        copies = []
        for i in range(half):
            columns = pl.ds(pl.multiple_of((index ^ (half + i)) * piece, piece), piece)
            for j, ref in enumerate((query_ref, grad_ref)):
                place = far_ref.at[i, j]
                copy = pltpu.make_async_copy(ref.at[0, :, columns], place, far_sems.at[i, j])
                copy.start()
                copies.append(copy)
        for copy in first:
            copy.wait()
        state = held[...].astype(jnp.float32)
        inverse = lax.rsqrt(jnp.mean(state * state, axis=1, keepdims=True) + epsilon)
        out_ref[...] = (state * inverse * held_gain[...]).astype(jnp.bfloat16)
        for copy in copies:
            copy.wait()

    return call(
        kernel,
        [shape((rows, width)), shape((half, 2, targets, piece))],
        moved=4 * rows * width + 4 * targets * width,
        vmem=VMEM_BEGIN,
        in_specs=[ANY] * 4,
        out_specs=[VMEM] * 2,
        scratch_shapes=[
            pltpu.VMEM((rows, width), jnp.bfloat16),
            pltpu.VMEM((1, width), jnp.float32),
            pltpu.SemaphoreType.DMA((2,)),
            pltpu.SemaphoreType.DMA((half, 2)),
        ],
    )(enc_state, gain, queries, ctx_grad)


def split_heads(queries, ctx_grad, groups, replicas, tokens):
    rows, width = queries.shape[1:]
    piece = width // replicas
    count = sum(len(group) for group in groups)

    def kernel(query_ref, grad_ref, *refs):
        *out_refs, token_ref, sems = refs[len(tokens) :]
        index = lax.axis_index("dp")
        copies = []
        for group, out_ref in zip(groups, out_refs, strict=True):
            for i, k in enumerate(group):
                columns = pl.ds(pl.multiple_of((index ^ k) * piece, piece), piece)
                for j, ref in enumerate((query_ref, grad_ref)):
                    sem = sems.at[len(copies)]
                    copy = pltpu.make_async_copy(ref.at[0, :, columns], out_ref.at[i, j], sem)
                    copy.start()
                    copies.append(copy)
        mark(token_ref)
        for copy in copies:
            copy.wait()

    *shares, token = call(
        kernel,
        [shape((len(group), 2, rows, piece)) for group in groups] + [TOKEN],
        moved=8 * rows * width,
        in_specs=[ANY] * (2 + len(tokens)),
        out_specs=[VMEM] * (len(groups) + 1),
        scratch_shapes=[pltpu.SemaphoreType.DMA((2 * count,))],
    )(queries, ctx_grad, *tokens)
    return shares, token


def add_blocks(blocks, tokens=(), mem_len=None):
    rows, width = blocks[0].shape
    assert rows <= 256
    scalars = [] if mem_len is None else [mem_len]

    def kernel(*refs):
        total = refs[0][...]
        for ref in refs[1 : len(blocks)]:
            total = total + ref[...]
        out_ref = refs[-1]
        out_ref[:, :width] = total
        if scalars:
            columns = jnp.full((rows, LANES), refs[len(blocks)][0].astype(jnp.float32))
            out_ref[:, width:] = columns.astype(jnp.bfloat16)

    return call(
        kernel,
        shape((rows, width + LANES * len(scalars))),
        moved=8 * blocks[0].size,
        in_specs=[VMEM] * len(blocks) + [SMEM] * len(scalars) + [ANY] * len(tokens),
        out_specs=VMEM,
    )(*blocks, *scalars, *tokens)


def stack_rows(first, second, tokens):
    rows, width = first.shape

    def kernel(first_ref, second_ref, *refs):
        out_ref = refs[-1]
        out_ref[:rows] = first_ref[...]
        out_ref[rows:] = second_ref[...]

    return call(
        kernel,
        shape((2 * rows, width)),
        moved=8 * first.size,
        in_specs=[VMEM] * 2 + [ANY] * len(tokens),
        out_specs=VMEM,
    )(first, second, *tokens)


def join_heads(shares):
    replicas, rows, piece = shares.shape

    def kernel(share_ref, out_ref, token_ref, sems):
        copies = []
        for k in range(replicas):
            columns = pl.ds(k * piece, piece)
            copy = pltpu.make_async_copy(share_ref.at[k], out_ref.at[0, :, columns], sems.at[k])
            copy.start()
            copies.append(copy)
        mark(token_ref)
        for copy in copies:
            copy.wait()

    return call(
        kernel,
        [shape((1, rows, replicas * piece)), TOKEN],
        moved=4 * rows * replicas * piece,
        in_specs=[VMEM],
        out_specs=[ANY, VMEM],
        scratch_shapes=[pltpu.SemaphoreType.DMA((replicas,))],
    )(shares)


def hold_weights(w_key, w_value, tokens):
    steps = 4
    step = w_key.shape[1] // steps

    def kernel(wk_ref, wv_ref, *refs):
        *out_refs, token_ref, sems = refs[len(tokens) :]
        copies = []
        for i in range(steps):
            rows = pl.ds(i * step, step)
            for j, (ref, out_ref) in enumerate(zip((wk_ref, wv_ref), out_refs, strict=True)):
                copy = pltpu.make_async_copy(ref.at[0, rows], out_ref.at[0, rows], sems.at[i, j])
                copy.start()
                copies.append(copy)
        mark(token_ref)
        for copy in copies:
            copy.wait()

    *held, token = call(
        kernel,
        [shape(w_key.shape)] * 2 + [TOKEN],
        flops=COST_HOLD,
        moved=4 * w_key.size,
        vmem=36,
        in_specs=[ANY] * (2 + len(tokens)),
        out_specs=[ANY, ANY, VMEM],
        scratch_shapes=[pltpu.SemaphoreType.DMA((steps, 2))],
    )(w_key, w_value, *tokens)
    return held, token


def follow(block, tokens):
    def kernel(*refs):
        del refs

    return call(
        kernel,
        shape(block.shape, block.dtype),
        in_specs=[ANY] * (1 + len(tokens)),
        out_specs=ANY,
        input_output_aliases={0: 0},
    )(block, *tokens)


def project(memory, w_key, w_value):
    rows = memory.shape[0]
    depth, width = w_key.shape[1:]

    def kernel(memory_ref, wk_ref, wv_ref, key_ref, value_ref):
        key_ref[...] = dot(memory_ref[:, :depth], wk_ref[0]).astype(jnp.bfloat16)
        value_ref[...] = dot(memory_ref[:, :depth], wv_ref[0]).astype(jnp.bfloat16)

    return call(
        kernel,
        [shape((rows, width))] * 2,
        flops=4 * rows * depth * width,
        moved=4 * depth * width,
        in_specs=[VMEM] * 3,
        out_specs=[VMEM] * 2,
    )(memory, w_key, w_value)


def attend(memory, keys, values, shares, order, half):
    count = len(shares)
    rows = memory.shape[0] // count
    depth = memory.shape[1] - LANES
    width = keys.shape[1]
    targets = shares[0].shape[2]
    scale = HEAD_DIM ** (-0.5)
    heads = width // HEAD_DIM

    def kernel(memory_ref, key_ref, value_ref, *refs):
        share_refs = refs[:count]
        dk_ref, dv_ref, dq_ref, score_ref, grad_ref, low_ref = refs[count:]
        index = lax.axis_index("dp")
        blocks = []
        for h in range(heads):
            for p, k in enumerate(order):
                head, own = slice(h * HEAD_DIM, (h + 1) * HEAD_DIM), slice(p * rows, (p + 1) * rows)
                blocks.append((head, own, index ^ k, share_refs[p]))
        for i, (head, own, _, share_ref) in enumerate(blocks):
            query, grad = share_ref[0, 0, :, head], share_ref[0, 1, :, head]
            score_ref[i] = dot(key_ref[own, head], query, ((1,), (1,)))
            grad_ref[i] = dot(value_ref[own, head], grad, ((1,), (1,)))
        token = lax.broadcasted_iota(jnp.int32, (rows, targets), 0).astype(jnp.float32)
        firsts = [memory_ref[p * rows : p * rows + 1, depth : depth + 1] for p in range(count)]
        valid = jnp.stack([token < first.astype(jnp.float32) for first in firsts])
        for h in range(heads):
            here = slice(h * count, (h + 1) * count)
            scores = jnp.where(valid, score_ref[here] * scale, -1e30)
            exponent = jnp.exp(scores - jnp.max(scores, axis=1, keepdims=True))
            probs = exponent / jnp.sum(exponent, axis=1, keepdims=True)
            grad_probs = grad_ref[here]
            delta = jnp.sum(probs * grad_probs, axis=1, keepdims=True)
            low_ref[0, here] = (probs * (grad_probs - delta) * scale).astype(jnp.bfloat16)
            low_ref[1, here] = probs.astype(jnp.bfloat16)
        is_decoder = (lax.axis_index("section") >= half).astype(jnp.float32)
        for i, (head, own, place, share_ref) in enumerate(blocks):
            query, grad = share_ref[0, 0, :, head], share_ref[0, 1, :, head]
            dk_ref[own, head] = dot(low_ref[0, i], query).astype(jnp.bfloat16)
            dv_ref[own, head] = (dot(low_ref[1, i], grad) * is_decoder).astype(jnp.bfloat16)
            dq = dot(low_ref[0, i], key_ref[own, head], ((0,), (0,)))
            dq_ref[place, :, head] = dq.astype(jnp.bfloat16)

    scores = (heads * count, rows, targets)
    return call(
        kernel,
        [shape((count * rows, width))] * 2 + [shape((count, targets, width))],
        flops=10 * count * rows * targets * width,
        moved=8 * count * targets * width,
        in_specs=[VMEM] * (count + 3),
        out_specs=[VMEM] * 3,
        scratch_shapes=[
            *[pltpu.VMEM(scores, jnp.float32)] * 2,
            pltpu.VMEM((2, *scores), jnp.bfloat16),
        ],
    )(memory, keys, values, *shares)


def memory_part(memory, w_key, w_value, dk, dv, gain):
    rows = memory.shape[0]
    depth, width = w_key.shape[1:]
    tile = 512
    steps = depth // tile
    keep = rows // 2

    def kernel(memory_ref, dk_ref, dv_ref, wk_ref, wv_ref, gain_ref, keep_ref, sent_ref, out_ref):
        for f in range(steps):
            here = slice(f * tile, (f + 1) * tile)
            part = dot(wk_ref[0, here, :], dk_ref[...], ((1,), (1,)))
            part = (part + dot(wv_ref[0, here, :], dv_ref[...], ((1,), (1,)))).T
            keep_ref[:, here] = part[:keep]
            sent_ref[:, here] = part[keep:].astype(jnp.bfloat16)
            terms = part * memory_ref[:, here].astype(jnp.float32)
            total = jnp.sum(terms, axis=0, keepdims=True) / gain_ref[:, here]
            for i in range(tile // LANES):
                place = (f * tile) // LANES + i
                out_ref[place : place + 1, :] = total[:, i * LANES : (i + 1) * LANES]
        put_gain(out_ref[...], sent_ref)

    return call(
        kernel,
        [
            shape((keep, depth), jnp.float32),
            shape((keep, depth + 2 * LANES)),
            shape((depth // LANES, LANES), jnp.float32),
        ],
        flops=4 * rows * depth * width,
        moved=4 * depth * width,
        in_specs=[VMEM] * 6,
        out_specs=[VMEM] * 3,
    )(memory, dk, dv, w_key, w_value, gain)


def put_gain(gain, sent_ref):
    rows = gain.shape[0]
    depth = sent_ref.shape[1] - 2 * LANES
    assert sent_ref.shape[0] >= rows
    high = gain.astype(jnp.bfloat16)
    if sent_ref.shape[0] > rows:
        sent_ref[rows:, depth:] = jnp.zeros((sent_ref.shape[0] - rows, 2 * LANES), jnp.bfloat16)
    sent_ref[:rows, depth : depth + LANES] = high
    sent_ref[:rows, depth + LANES :] = (gain - high.astype(jnp.float32)).astype(jnp.bfloat16)


def add_share(kept, came, gain, last, tokens=()):
    rows, depth = kept.shape
    half = rows if last else rows // 2

    def kernel(kept_ref, came_ref, gain_ref, *refs):
        sent_ref, out_ref, *more_refs = refs[len(tokens) :]
        out = gain_ref.shape[0]
        came_gain = came_ref[:out, depth:].astype(jnp.float32)
        total_gain = gain_ref[...] + (came_gain[:, :LANES] + came_gain[:, LANES:])
        out_ref[...] = total_gain
        total = kept_ref[:half] + came_ref[:half, :depth].astype(jnp.float32)
        if last:
            sent_ref[...] = total.astype(jnp.bfloat16)
        else:
            keep_ref, token_ref = more_refs
            keep_ref[...] = total
            other = kept_ref[half:] + came_ref[half:, :depth].astype(jnp.float32)
            sent_ref[:, :depth] = other.astype(jnp.bfloat16)
            put_gain(total_gain, sent_ref)
            mark(token_ref)

    more = [] if last else [shape((half, depth), jnp.float32), TOKEN]
    return call(
        kernel,
        [
            shape((half, depth + (0 if last else 2 * LANES))),
            shape(gain.shape, jnp.float32),
            *more,
        ],
        moved=10 * rows * depth,
        in_specs=[VMEM] * 3 + [ANY] * len(tokens),
        out_specs=[VMEM] * (2 + len(more)),
    )(kept, came, gain, *tokens)


def add_sections(own, came, gain):
    count = len(came)

    def kernel(own_ref, *refs):
        gain_ref = refs[count]
        out_ref, gain_out_ref = refs[-2:]
        total = own_ref[...].astype(jnp.float32)
        for ref in refs[:count]:
            total = total + ref[...].astype(jnp.float32)
        out_ref[...] = total.astype(jnp.bfloat16)
        gain_out_ref[...] = gain_ref[...]

    return call(
        kernel,
        [shape(own.shape), shape(gain.shape, jnp.float32)],
        flops=COST_SUM,
        moved=6 * own.size,
        in_specs=[VMEM] * (2 + count),
        out_specs=[VMEM] * 2,
    )(own, *came, gain)


def add_gains(terms, token):
    def kernel(own_ref, other_ref, first_ref, second_ref, _, out_ref):
        out_ref[...] = (own_ref[...] + other_ref[...]) + (first_ref[...] + second_ref[...])

    return call(
        kernel,
        shape(terms[0].shape, jnp.float32),
        in_specs=[VMEM] * 4 + [ANY],
        out_specs=VMEM,
    )(*terms, token)


def weight_grads(memory, width, first, last, dk, dv, before, tokens=()):
    rows = memory.shape[0]
    columns = dk.shape[1]
    tile = TILE

    def kernel(memory_ref, dk_ref, dv_ref, *refs):
        key_ref, value_ref, token_ref = refs[-3:]
        key_ref[0] = dot(memory_ref[...], dk_ref[...], ((0,), (0,))).astype(jnp.bfloat16)
        value_ref[0] = dot(memory_ref[...], dv_ref[...], ((0,), (0,))).astype(jnp.bfloat16)
        mark(token_ref)

    piece = pl.BlockSpec((rows, tile), lambda f: (0, first + f))
    whole = pl.BlockSpec((rows, columns), lambda f: (0, 0))
    out = pl.BlockSpec((1, tile, columns), lambda f: (0, first + f, 0))
    inputs = 3 + len(tokens)
    *grads, token = call(
        kernel,
        [shape((1, width, columns))] * 2 + [TOKEN],
        flops=4 * rows * tile * columns * (last - first),
        moved=4 * tile * columns * (last - first),
        grid=(last - first,),
        in_specs=[piece, whole, whole] + [ANY] * (len(tokens) + len(before)),
        out_specs=[out] * 2 + [pl.BlockSpec(TOKEN.shape, lambda f: (0, 0))],
        vmem=24,
        input_output_aliases={inputs + i: i for i in range(len(before))},
    )(memory, dk, dv, *tokens, *before)
    return grads, token


def finish(holder, enc_state, gain, terms, tokens):
    rows, width = enc_state.shape[1:]

    def kernel(enc_ref, gain_ref, *refs):
        state = enc_ref[0].astype(jnp.float32)
        inverse = lax.rsqrt(jnp.mean(state * state, axis=1, keepdims=True) + epsilon)
        normed = state * inverse
        own = [ref[...].astype(jnp.float32) for ref in refs[: len(terms)]]
        scaled = sum(own[1:], own[0]) * gain_ref[...]
        mean = jnp.mean(scaled * normed, axis=1, keepdims=True)
        grad = inverse * (scaled - normed * mean)
        is_holder = lax.axis_index("section") == holder
        refs[-2][0] = jnp.where(is_holder, grad, 0.0).astype(jnp.bfloat16)
        mark(refs[-1])

    return call(
        kernel,
        [shape((1, rows, width)), TOKEN],
        moved=8 * rows * width,
        in_specs=[VMEM] * (2 + len(terms)) + [ANY] * len(tokens),
        out_specs=[VMEM] * 2,
    )(enc_state, gain, *terms, *tokens)


def on_device(enc_state, final_gain, queries, w_key, w_value, ctx_grad, mem_len):
    sections = lax.axis_size("section")
    replicas = lax.axis_size("dp")
    half = sections // 2
    bits = replicas.bit_length() - 1
    assert replicas == 1 << bits and half & (half - 1) == 0 and half > 1 and bits > 1
    gain = final_gain[None]

    def over_dp(block, k):
        pairs = [
            (s * replicas + d, s * replicas + (d ^ k))
            for s in range(half, sections)
            for d in range(replicas)
        ]
        return lax.ppermute(block, BOTH, pairs)

    def over_section(block, pairs):
        pairs = [(a * replicas + d, b * replicas + d) for a, b in pairs for d in range(replicas)]
        return lax.ppermute(block, BOTH, pairs)

    order = [0]
    for bit in reversed(range(bits)):
        order = order + [k ^ (1 << bit) for k in order]
    rounds = section_rounds(sections)

    memory, far = begin(enc_state, gain, queries, ctx_grad, replicas)
    came_far = over_dp(far, replicas // 2)
    groups = [[k for k in range(1 << bit, 2 << bit)] for bit in reversed(range(bits - 1))]
    near, split = split_heads(queries, ctx_grad, [*groups, [0]], replicas, [])
    came = [over_section(memory, group) for group in split_pairs(rounds[0])]
    arrived = [came[0]]
    holding = add_blocks(came, [split])
    weights, held = hold_weights(w_key, w_value, [holding])
    for stage in rounds[1:]:
        arrived += [over_section(holding, group) for group in split_pairs(stage)]
        length = mem_len if stage is rounds[-1] else None
        holding = add_blocks(arrived, [held], length)
    blocks, tokens = {replicas // 2: came_far}, []
    for bit, share in zip(reversed(range(bits - 1)), near, strict=False):
        size = 1 << bit
        passed = {k ^ size: over_dp(b[size : 2 * size], size) for k, b in blocks.items()}
        blocks = blocks | passed | {size: over_dp(share, size)}
        tokens.append(blocks[size])
    blocks[0] = near[-1]
    shares = [blocks[k] for k in order]
    for bit in reversed(range(bits)):
        holding = stack_rows(holding, over_dp(holding, 1 << bit), tokens)
        tokens = []
    pieces = holding
    keys, values = project(pieces, *weights)
    dk, dv, dq = attend(pieces, keys, values, shares, order, half)

    kept, sent, gain_part = memory_part(pieces, *weights, dk, dv, gain)
    width = enc_state.shape[2]
    decoders = range(half, sections)
    token = None
    for bit in range(bits):
        last = bit == bits - 1
        came = over_dp(sent, 1 << bit)
        tokens = []
        if last:
            grads, done = weight_grads(pieces, width, 0, width // TILE, dk, dv, [], [token])
            tokens = [done]
        sent, gain_part, *more = add_share(kept, came, gain_part, last, tokens)
        if not last:
            kept, token = more
    key_weight_grad, value_weight_grad = grads
    dq = follow(dq, [gain_part])
    step = half // 2
    while step > 1:
        gain_part = gain_part + over_section(gain_part, [(s, s ^ step) for s in decoders])
        step //= 2
    for number, stage in reversed(list(enumerate(rounds))):
        came = [over_section(sent, [(b, a) for a, b in group]) for group in split_pairs(stage)]
        if number:
            sent, gain_part = add_sections(sent, came, gain_part)
    terms = [
        gain_part,
        over_section(gain_part, [(s, s ^ step) for s in decoders]),
        over_section(gain_part, [(s, s - half) for s in decoders]),
        over_section(gain_part, [(s, (s ^ step) - half) for s in decoders]),
    ]

    query_grad, joined = join_heads(
        lax.all_to_all(dq, "dp", split_axis=0, concat_axis=0, tiled=True)
    )
    state_grad, done = finish(half - 1, enc_state, gain, came, [joined])
    gain_grad = add_gains(terms, done).reshape(width)
    return (query_grad, key_weight_grad, value_weight_grad, state_grad, gain_grad)


def solution(mesh):
    placed = (
        P("section", "dp", None),
        P(),
        P("section", "dp", None),
        P("section", None, "dp"),
        P("section", None, "dp"),
        P("section", "dp", None),
        P("dp"),
    )
    return jax.shard_map(
        on_device,
        mesh=mesh,
        in_specs=placed,
        out_specs=(
            P("section", "dp", None),
            P("section", None, "dp"),
            P("section", None, "dp"),
            P("section", "dp", None),
            P(),
        ),
        check_vma=False,
    )
```

```python
import jax
import jax.numpy as jnp
from jax import lax
from jax.experimental import pallas as pl
from jax.experimental.pallas import tpu as pltpu
from jax.sharding import PartitionSpec as P

HEAD_DIM = 256
epsilon = 1e-06
BOTH = ("section", "dp")
LANES = 128
TILE = 1024
VMEM_BEGIN = 54
COST_HOLD = 1 << 30
COST_SUM = 1 << 32


def section_rounds(sections):
    half = sections // 2
    source = half - 1
    first = min(half + 1, sections - 1)
    held = {source, first}
    rounds = [[(source, first)]]
    if source > 0 and half + 2 < sections:
        rounds[0].append((source, source - 1))
        held.add(source - 1)
    stage = []
    for a, b in ((first, first + 2), (source - 1, source + 3), (first, first - 1)):
        if a in held and half <= b < sections and b not in held:
            stage.append((a, b))
            held.add(b)
    if stage:
        rounds.append(stage)
    while not held.issuperset(range(half, sections)):
        have = [s for s in sorted(held) if s >= half]
        stage = []
        for a in have:
            b = a + len(have)
            if b < sections and b not in held:
                stage.append((a, b))
                held.add(b)
        rounds.append(stage)
    return rounds


def split_pairs(stage):
    groups = []
    for a, b in stage:
        for group in groups:
            if all(a != c and b != e for c, e in group):
                group.append((a, b))
                break
        else:
            groups.append([(a, b)])
    return groups


def call(kernel, out_shape, flops=0, moved=0, vmem=16, **options):
    return pl.pallas_call(
        kernel,
        out_shape=out_shape,
        compiler_params=pltpu.CompilerParams(vmem_limit_bytes=vmem << 20),
        cost_estimate=pl.CostEstimate(flops=flops, bytes_accessed=moved, transcendentals=0),
        **options,
    )


def shape(dims, dtype=jnp.bfloat16):
    return jax.ShapeDtypeStruct(dims, dtype)


def dot(a, b, dims=((1,), (0,))):
    return lax.dot_general(a, b, (dims, ((), ())), preferred_element_type=jnp.float32)


SMEM = pl.BlockSpec(memory_space=pltpu.SMEM)
VMEM = pl.BlockSpec(memory_space=pltpu.VMEM)
ANY = pl.BlockSpec(memory_space=pl.ANY)
TOKEN = shape((8, LANES), jnp.float32)


def mark(token_ref):
    token_ref[...] = jnp.zeros_like(token_ref)


def begin(enc_state, gain, queries, ctx_grad, replicas):
    rows, width = enc_state.shape[1:]
    targets = queries.shape[1]
    piece = width // replicas
    half = replicas // 2

    def kernel(enc_ref, gain_ref, query_ref, grad_ref, *refs):
        out_ref, far_ref, token_ref, held, held_gain, sems, far_sems = refs
        mark(token_ref)
        first = [
            pltpu.make_async_copy(enc_ref.at[0], held, sems.at[0]),
            pltpu.make_async_copy(gain_ref, held_gain, sems.at[1]),
        ]
        for copy in first:
            copy.start()
        index = lax.axis_index("dp")
        copies = []
        for i in range(half):
            columns = pl.ds(pl.multiple_of((index ^ (half + i)) * piece, piece), piece)
            for j, ref in enumerate((query_ref, grad_ref)):
                place = far_ref.at[i, j]
                copy = pltpu.make_async_copy(ref.at[0, :, columns], place, far_sems.at[i, j])
                copy.start()
                copies.append(copy)
        for copy in first:
            copy.wait()
        state = held[...].astype(jnp.float32)
        inverse = lax.rsqrt(jnp.mean(state * state, axis=1, keepdims=True) + epsilon)
        out_ref[...] = (state * inverse * held_gain[...]).astype(jnp.bfloat16)
        for copy in copies:
            copy.wait()

    return call(
        kernel,
        [shape((rows, width)), shape((half, 2, targets, piece)), TOKEN],
        moved=4 * rows * width + 4 * targets * width,
        vmem=VMEM_BEGIN,
        in_specs=[ANY] * 4,
        out_specs=[VMEM] * 3,
        scratch_shapes=[
            pltpu.VMEM((rows, width), jnp.bfloat16),
            pltpu.VMEM((1, width), jnp.float32),
            pltpu.SemaphoreType.DMA((2,)),
            pltpu.SemaphoreType.DMA((half, 2)),
        ],
    )(enc_state, gain, queries, ctx_grad)


def split_heads(queries, ctx_grad, groups, replicas, tokens):
    rows, width = queries.shape[1:]
    piece = width // replicas
    count = sum(len(group) for group in groups)

    def kernel(query_ref, grad_ref, *refs):
        *out_refs, token_ref, sems = refs[len(tokens) :]
        index = lax.axis_index("dp")
        copies = []
        for group, out_ref in zip(groups, out_refs, strict=True):
            for i, k in enumerate(group):
                columns = pl.ds(pl.multiple_of((index ^ k) * piece, piece), piece)
                for j, ref in enumerate((query_ref, grad_ref)):
                    sem = sems.at[len(copies)]
                    copy = pltpu.make_async_copy(ref.at[0, :, columns], out_ref.at[i, j], sem)
                    copy.start()
                    copies.append(copy)
        mark(token_ref)
        for copy in copies:
            copy.wait()

    *shares, token = call(
        kernel,
        [shape((len(group), 2, rows, piece)) for group in groups] + [TOKEN],
        moved=8 * rows * width,
        in_specs=[ANY] * (2 + len(tokens)),
        out_specs=[VMEM] * (len(groups) + 1),
        scratch_shapes=[pltpu.SemaphoreType.DMA((2 * count,))],
    )(queries, ctx_grad, *tokens)
    return shares, token


def add_blocks(blocks, tokens=(), mem_len=None):
    rows, width = blocks[0].shape
    assert rows <= 256
    scalars = [] if mem_len is None else [mem_len]

    def kernel(*refs):
        total = refs[0][...]
        for ref in refs[1 : len(blocks)]:
            total = total + ref[...]
        out_ref = refs[-1]
        out_ref[:, :width] = total
        if scalars:
            columns = jnp.full((rows, LANES), refs[len(blocks)][0].astype(jnp.float32))
            out_ref[:, width:] = columns.astype(jnp.bfloat16)

    return call(
        kernel,
        shape((rows, width + LANES * len(scalars))),
        moved=8 * blocks[0].size,
        in_specs=[VMEM] * len(blocks) + [SMEM] * len(scalars) + [ANY] * len(tokens),
        out_specs=VMEM,
    )(*blocks, *scalars, *tokens)


def stack_rows(first, second, tokens):
    rows, width = first.shape

    def kernel(first_ref, second_ref, *refs):
        out_ref = refs[-1]
        out_ref[:rows] = first_ref[...]
        out_ref[rows:] = second_ref[...]

    return call(
        kernel,
        shape((2 * rows, width)),
        moved=8 * first.size,
        in_specs=[VMEM] * 2 + [ANY] * len(tokens),
        out_specs=VMEM,
    )(first, second, *tokens)


def join_heads(shares):
    replicas, rows, piece = shares.shape

    def kernel(share_ref, out_ref, token_ref, sems):
        copies = []
        for k in range(replicas):
            columns = pl.ds(k * piece, piece)
            copy = pltpu.make_async_copy(share_ref.at[k], out_ref.at[0, :, columns], sems.at[k])
            copy.start()
            copies.append(copy)
        mark(token_ref)
        for copy in copies:
            copy.wait()

    return call(
        kernel,
        [shape((1, rows, replicas * piece)), TOKEN],
        moved=4 * rows * replicas * piece,
        in_specs=[VMEM],
        out_specs=[ANY, VMEM],
        scratch_shapes=[pltpu.SemaphoreType.DMA((replicas,))],
    )(shares)


def hold_weights(w_key, w_value, tokens):
    steps = 4
    step = w_key.shape[1] // steps

    def kernel(wk_ref, wv_ref, *refs):
        *out_refs, token_ref, sems = refs[len(tokens) :]
        copies = []
        for i in range(steps):
            rows = pl.ds(i * step, step)
            for j, (ref, out_ref) in enumerate(zip((wk_ref, wv_ref), out_refs, strict=True)):
                copy = pltpu.make_async_copy(ref.at[0, rows], out_ref.at[0, rows], sems.at[i, j])
                copy.start()
                copies.append(copy)
        mark(token_ref)
        for copy in copies:
            copy.wait()

    *held, token = call(
        kernel,
        [shape(w_key.shape)] * 2 + [TOKEN],
        flops=COST_HOLD,
        moved=4 * w_key.size,
        vmem=36,
        in_specs=[ANY] * (2 + len(tokens)),
        out_specs=[ANY, ANY, VMEM],
        scratch_shapes=[pltpu.SemaphoreType.DMA((steps, 2))],
    )(w_key, w_value, *tokens)
    return held, token


def project(memory, w_key, w_value):
    rows = memory.shape[0]
    depth, width = w_key.shape[1:]

    def kernel(memory_ref, wk_ref, wv_ref, key_ref, value_ref):
        key_ref[...] = dot(memory_ref[:, :depth], wk_ref[0]).astype(jnp.bfloat16)
        value_ref[...] = dot(memory_ref[:, :depth], wv_ref[0]).astype(jnp.bfloat16)

    return call(
        kernel,
        [shape((rows, width))] * 2,
        flops=4 * rows * depth * width,
        moved=4 * depth * width,
        in_specs=[VMEM] * 3,
        out_specs=[VMEM] * 2,
    )(memory, w_key, w_value)


def attend(memory, keys, values, shares, half):
    count = len(shares)
    rows = memory.shape[0] // count
    depth = memory.shape[1] - LANES
    width = keys.shape[1]
    targets = shares[0].shape[2]
    scale = HEAD_DIM ** (-0.5)
    heads = width // HEAD_DIM

    def kernel(memory_ref, key_ref, value_ref, *refs):
        share_refs = refs[:count]
        dk_ref, dv_ref, low_ref, score_ref, grad_ref = refs[count:]
        blocks = []
        for h in range(heads):
            for p in range(count):
                head, own = slice(h * HEAD_DIM, (h + 1) * HEAD_DIM), slice(p * rows, (p + 1) * rows)
                blocks.append((head, own, share_refs[p]))
        for i, (head, own, share_ref) in enumerate(blocks):
            query, grad = share_ref[0, 0, :, head], share_ref[0, 1, :, head]
            score_ref[i] = dot(key_ref[own, head], query, ((1,), (1,)))
            grad_ref[i] = dot(value_ref[own, head], grad, ((1,), (1,)))
        token = lax.broadcasted_iota(jnp.int32, (rows, targets), 0).astype(jnp.float32)
        firsts = [memory_ref[p * rows : p * rows + 1, depth : depth + 1] for p in range(count)]
        valid = jnp.stack([token < first.astype(jnp.float32) for first in firsts])
        for h in range(heads):
            here = slice(h * count, (h + 1) * count)
            scores = jnp.where(valid, score_ref[here] * scale, -1e30)
            exponent = jnp.exp(scores - jnp.max(scores, axis=1, keepdims=True))
            probs = exponent / jnp.sum(exponent, axis=1, keepdims=True)
            grad_probs = grad_ref[here]
            delta = jnp.sum(probs * grad_probs, axis=1, keepdims=True)
            low_ref[0, here] = (probs * (grad_probs - delta) * scale).astype(jnp.bfloat16)
            low_ref[1, here] = probs.astype(jnp.bfloat16)
        is_decoder = (lax.axis_index("section") >= half).astype(jnp.float32)
        for i, (head, own, share_ref) in enumerate(blocks):
            query, grad = share_ref[0, 0, :, head], share_ref[0, 1, :, head]
            dk_ref[own, head] = dot(low_ref[0, i], query).astype(jnp.bfloat16)
            dv_ref[own, head] = (dot(low_ref[1, i], grad) * is_decoder).astype(jnp.bfloat16)

    scores = (heads * count, rows, targets)
    return call(
        kernel,
        [shape((count * rows, width))] * 2 + [shape((2, *scores))],
        flops=8 * count * rows * targets * width,
        moved=8 * count * targets * width,
        in_specs=[VMEM] * (count + 3),
        out_specs=[VMEM] * 3,
        scratch_shapes=[
            *[pltpu.VMEM(scores, jnp.float32)] * 2,
        ],
    )(memory, keys, values, *shares)


def query_grads(scores, keys, order, tokens):
    count = len(order)
    rows = keys.shape[0] // count
    width = keys.shape[1]
    targets = scores.shape[3]

    def kernel(score_ref, key_ref, *refs):
        out_ref = refs[-1]
        index = lax.axis_index("dp")
        for h in range(width // HEAD_DIM):
            head = slice(h * HEAD_DIM, (h + 1) * HEAD_DIM)
            for p, k in enumerate(order):
                key = key_ref[p * rows : (p + 1) * rows, head]
                grad = dot(score_ref[0, h * count + p], key, ((0,), (0,)))
                out_ref[index ^ k, :, head] = grad.astype(jnp.bfloat16)

    return call(
        kernel,
        shape((count, targets, width)),
        flops=2 * count * rows * targets * width,
        moved=4 * count * targets * width,
        in_specs=[VMEM] * 2 + [ANY] * len(tokens),
        out_specs=VMEM,
    )(scores, keys, *tokens)


def memory_part(memory, w_key, w_value, dk, dv, gain):
    rows = memory.shape[0]
    depth, width = w_key.shape[1:]
    tile = 512
    steps = depth // tile
    keep = rows // 2

    def kernel(memory_ref, dk_ref, dv_ref, wk_ref, wv_ref, gain_ref, keep_ref, sent_ref, out_ref):
        for f in range(steps):
            here = slice(f * tile, (f + 1) * tile)
            part = dot(wk_ref[0, here, :], dk_ref[...], ((1,), (1,)))
            part = (part + dot(wv_ref[0, here, :], dv_ref[...], ((1,), (1,)))).T
            keep_ref[:, here] = part[:keep]
            sent_ref[:, here] = part[keep:].astype(jnp.bfloat16)
            terms = part * memory_ref[:, here].astype(jnp.float32)
            total = jnp.sum(terms, axis=0, keepdims=True) / gain_ref[:, here]
            for i in range(tile // LANES):
                place = (f * tile) // LANES + i
                out_ref[place : place + 1, :] = total[:, i * LANES : (i + 1) * LANES]
        put_gain(out_ref[...], sent_ref)

    return call(
        kernel,
        [
            shape((keep, depth), jnp.float32),
            shape((keep, depth + 2 * LANES)),
            shape((depth // LANES, LANES), jnp.float32),
        ],
        flops=4 * rows * depth * width,
        moved=4 * depth * width,
        in_specs=[VMEM] * 6,
        out_specs=[VMEM] * 3,
    )(memory, dk, dv, w_key, w_value, gain)


def put_gain(gain, sent_ref):
    rows = gain.shape[0]
    depth = sent_ref.shape[1] - 2 * LANES
    assert sent_ref.shape[0] >= rows
    high = gain.astype(jnp.bfloat16)
    if sent_ref.shape[0] > rows:
        sent_ref[rows:, depth:] = jnp.zeros((sent_ref.shape[0] - rows, 2 * LANES), jnp.bfloat16)
    sent_ref[:rows, depth : depth + LANES] = high
    sent_ref[:rows, depth + LANES :] = (gain - high.astype(jnp.float32)).astype(jnp.bfloat16)


def add_share(kept, came, gain, last, tokens=()):
    rows, depth = kept.shape
    half = rows if last else rows // 2

    def kernel(kept_ref, came_ref, gain_ref, *refs):
        sent_ref, out_ref, *more_refs = refs[len(tokens) :]
        out = gain_ref.shape[0]
        came_gain = came_ref[:out, depth:].astype(jnp.float32)
        total_gain = gain_ref[...] + (came_gain[:, :LANES] + came_gain[:, LANES:])
        out_ref[...] = total_gain
        total = kept_ref[:half] + came_ref[:half, :depth].astype(jnp.float32)
        if last:
            sent_ref[...] = total.astype(jnp.bfloat16)
        else:
            keep_ref, token_ref = more_refs
            keep_ref[...] = total
            other = kept_ref[half:] + came_ref[half:, :depth].astype(jnp.float32)
            sent_ref[:, :depth] = other.astype(jnp.bfloat16)
            put_gain(total_gain, sent_ref)
            mark(token_ref)

    more = [] if last else [shape((half, depth), jnp.float32), TOKEN]
    return call(
        kernel,
        [
            shape((half, depth + (0 if last else 2 * LANES))),
            shape(gain.shape, jnp.float32),
            *more,
        ],
        moved=10 * rows * depth,
        in_specs=[VMEM] * 3 + [ANY] * len(tokens),
        out_specs=[VMEM] * (2 + len(more)),
    )(kept, came, gain, *tokens)


def add_sections(own, came, gain):
    count = len(came)

    def kernel(own_ref, *refs):
        gain_ref = refs[count]
        out_ref, gain_out_ref = refs[-2:]
        total = own_ref[...].astype(jnp.float32)
        for ref in refs[:count]:
            total = total + ref[...].astype(jnp.float32)
        out_ref[...] = total.astype(jnp.bfloat16)
        gain_out_ref[...] = gain_ref[...]

    return call(
        kernel,
        [shape(own.shape), shape(gain.shape, jnp.float32)],
        flops=COST_SUM,
        moved=6 * own.size,
        in_specs=[VMEM] * (2 + count),
        out_specs=[VMEM] * 2,
    )(own, *came, gain)


def add_gains(terms, token):
    def kernel(own_ref, other_ref, first_ref, second_ref, _, out_ref):
        out_ref[...] = (own_ref[...] + other_ref[...]) + (first_ref[...] + second_ref[...])

    return call(
        kernel,
        shape(terms[0].shape, jnp.float32),
        in_specs=[VMEM] * 4 + [ANY],
        out_specs=VMEM,
    )(*terms, token)


def weight_grads(memory, width, first, last, dk, dv, before, tokens=()):
    rows = memory.shape[0]
    columns = dk.shape[1]
    tile = TILE

    def kernel(memory_ref, dk_ref, dv_ref, *refs):
        key_ref, value_ref, token_ref = refs[-3:]
        key_ref[0] = dot(memory_ref[...], dk_ref[...], ((0,), (0,))).astype(jnp.bfloat16)
        value_ref[0] = dot(memory_ref[...], dv_ref[...], ((0,), (0,))).astype(jnp.bfloat16)
        mark(token_ref)

    piece = pl.BlockSpec((rows, tile), lambda f: (0, first + f))
    whole = pl.BlockSpec((rows, columns), lambda f: (0, 0))
    out = pl.BlockSpec((1, tile, columns), lambda f: (0, first + f, 0))
    inputs = 3 + len(tokens)
    *grads, token = call(
        kernel,
        [shape((1, width, columns))] * 2 + [TOKEN],
        flops=4 * rows * tile * columns * (last - first),
        moved=4 * tile * columns * (last - first),
        grid=(last - first,),
        in_specs=[piece, whole, whole] + [ANY] * (len(tokens) + len(before)),
        out_specs=[out] * 2 + [pl.BlockSpec(TOKEN.shape, lambda f: (0, 0))],
        vmem=24,
        input_output_aliases={inputs + i: i for i in range(len(before))},
    )(memory, dk, dv, *tokens, *before)
    return grads, token


def finish(holder, enc_state, gain, terms, tokens):
    rows, width = enc_state.shape[1:]

    def kernel(enc_ref, gain_ref, *refs):
        state = enc_ref[0].astype(jnp.float32)
        inverse = lax.rsqrt(jnp.mean(state * state, axis=1, keepdims=True) + epsilon)
        normed = state * inverse
        own = [ref[...].astype(jnp.float32) for ref in refs[: len(terms)]]
        scaled = sum(own[1:], own[0]) * gain_ref[...]
        mean = jnp.mean(scaled * normed, axis=1, keepdims=True)
        grad = inverse * (scaled - normed * mean)
        is_holder = lax.axis_index("section") == holder
        refs[-2][0] = jnp.where(is_holder, grad, 0.0).astype(jnp.bfloat16)
        mark(refs[-1])

    return call(
        kernel,
        [shape((1, rows, width)), TOKEN],
        moved=8 * rows * width,
        in_specs=[VMEM] * (2 + len(terms)) + [ANY] * len(tokens),
        out_specs=[VMEM] * 2,
    )(enc_state, gain, *terms, *tokens)


def on_device(enc_state, final_gain, queries, w_key, w_value, ctx_grad, mem_len):
    sections = lax.axis_size("section")
    replicas = lax.axis_size("dp")
    half = sections // 2
    bits = replicas.bit_length() - 1
    assert replicas == 1 << bits and half & (half - 1) == 0 and half > 1 and bits > 1
    gain = final_gain[None]

    def over_dp(block, k):
        pairs = [
            (s * replicas + d, s * replicas + (d ^ k))
            for s in range(half, sections)
            for d in range(replicas)
        ]
        return lax.ppermute(block, BOTH, pairs)

    def over_section(block, pairs):
        pairs = [(a * replicas + d, b * replicas + d) for a, b in pairs for d in range(replicas)]
        return lax.ppermute(block, BOTH, pairs)

    order = [0]
    for bit in reversed(range(bits)):
        order = order + [k ^ (1 << bit) for k in order]
    rounds = section_rounds(sections)

    memory, far, begun = begin(enc_state, gain, queries, ctx_grad, replicas)
    came_far = over_dp(far, replicas // 2)
    groups = [[k for k in range(1 << bit, 2 << bit)] for bit in reversed(range(bits - 1))]
    came = [over_section(memory, group) for group in split_pairs(rounds[0])]
    arrived = [came[0]]
    weights, held = hold_weights(w_key, w_value, [begun])
    holding = add_blocks(came, [held])
    near, split = split_heads(queries, ctx_grad, [*groups, [0]], replicas, [holding])
    for stage in rounds[1:]:
        arrived += [over_section(holding, group) for group in split_pairs(stage)]
        length = mem_len if stage is rounds[-1] else None
        holding = add_blocks(arrived, [split], length)
    blocks, tokens = {replicas // 2: came_far}, []
    for bit, share in zip(reversed(range(bits - 1)), near, strict=False):
        size = 1 << bit
        passed = {k ^ size: over_dp(b[size : 2 * size], size) for k, b in blocks.items()}
        blocks = blocks | passed | {size: over_dp(share, size)}
        tokens.append(blocks[size])
    blocks[0] = near[-1]
    shares = [blocks[k] for k in order]
    for bit in reversed(range(bits)):
        holding = stack_rows(holding, over_dp(holding, 1 << bit), tokens)
        tokens = []
    pieces = holding
    keys, values = project(pieces, *weights)
    dk, dv, scores = attend(pieces, keys, values, shares, half)

    kept, sent, gain_part = memory_part(pieces, *weights, dk, dv, gain)
    width = enc_state.shape[2]
    decoders = range(half, sections)
    token = None
    for bit in range(bits):
        last = bit == bits - 1
        came = over_dp(sent, 1 << bit)
        tokens = []
        if last:
            grads, done = weight_grads(pieces, width, 0, width // TILE, dk, dv, [], [token])
            tokens = [done]
        sent, gain_part, *more = add_share(kept, came, gain_part, last, tokens)
        if not last:
            kept, token = more
    key_weight_grad, value_weight_grad = grads
    dq = query_grads(scores, keys, order, [gain_part])
    step = 1
    while step < half // 2:
        gain_part = gain_part + over_section(gain_part, [(s, s ^ step) for s in decoders])
        step *= 2
    for number, stage in reversed(list(enumerate(rounds))):
        came = [over_section(sent, [(b, a) for a, b in group]) for group in split_pairs(stage)]
        if number:
            sent, gain_part = add_sections(sent, came, gain_part)
    places = [(i % step) * 2 + i // step for i in range(half)]
    terms = [
        gain_part,
        over_section(gain_part, [(s, s ^ step) for s in decoders]),
        over_section(gain_part, [(half + i, places[i]) for i in range(half)]),
        over_section(gain_part, [(half + i, places[i ^ step]) for i in range(half)]),
    ]

    query_grad, joined = join_heads(
        lax.all_to_all(dq, "dp", split_axis=0, concat_axis=0, tiled=True)
    )
    state_grad, done = finish(half - 1, enc_state, gain, came, [joined])
    gain_grad = add_gains(terms, done).reshape(width)
    return (query_grad, key_weight_grad, value_weight_grad, state_grad, gain_grad)


def solution(mesh):
    placed = (
        P("section", "dp", None),
        P(),
        P("section", "dp", None),
        P("section", None, "dp"),
        P("section", None, "dp"),
        P("section", "dp", None),
        P("dp"),
    )
    return jax.shard_map(
        on_device,
        mesh=mesh,
        in_specs=placed,
        out_specs=(
            P("section", "dp", None),
            P("section", None, "dp"),
            P("section", None, "dp"),
            P("section", "dp", None),
            P(),
        ),
        check_vma=False,
    )
```

```python
import jax
import jax.numpy as jnp
from jax import lax
from jax.experimental import pallas as pl
from jax.experimental.pallas import tpu as pltpu
from jax.sharding import PartitionSpec as P

HEAD_DIM = 256
epsilon = 1e-06
BOTH = ("section", "dp")
LANES = 128
TILE = 1024
VMEM_BEGIN = 54
COST_HOLD = 1 << 30
COST_SUM = 3 << 30
COST_GAIN = 1 << 32


def section_rounds(sections):
    half = sections // 2
    source = half - 1
    first = min(half + 1, sections - 1)
    held = {source, first}
    rounds = [[(source, first)]]
    if source > 0 and half + 2 < sections:
        rounds[0].append((source, source - 1))
        held.add(source - 1)
    stage = []
    for a, b in ((first, first + 2), (source - 1, source + 3), (first, first - 1)):
        if a in held and half <= b < sections and b not in held:
            stage.append((a, b))
            held.add(b)
    if stage:
        rounds.append(stage)
    while not held.issuperset(range(half, sections)):
        have = [s for s in sorted(held) if s >= half]
        stage = []
        for a in have:
            b = a + len(have)
            if b < sections and b not in held:
                stage.append((a, b))
                held.add(b)
        rounds.append(stage)
    return rounds


def split_pairs(stage):
    groups = []
    for a, b in stage:
        for group in groups:
            if all(a != c and b != e for c, e in group):
                group.append((a, b))
                break
        else:
            groups.append([(a, b)])
    return groups


def call(kernel, out_shape, flops=0, moved=0, vmem=16, **options):
    return pl.pallas_call(
        kernel,
        out_shape=out_shape,
        compiler_params=pltpu.CompilerParams(vmem_limit_bytes=vmem << 20),
        cost_estimate=pl.CostEstimate(flops=flops, bytes_accessed=moved, transcendentals=0),
        **options,
    )


def shape(dims, dtype=jnp.bfloat16):
    return jax.ShapeDtypeStruct(dims, dtype)


def dot(a, b, dims=((1,), (0,))):
    return lax.dot_general(a, b, (dims, ((), ())), preferred_element_type=jnp.float32)


SMEM = pl.BlockSpec(memory_space=pltpu.SMEM)
VMEM = pl.BlockSpec(memory_space=pltpu.VMEM)
ANY = pl.BlockSpec(memory_space=pl.ANY)
TOKEN = shape((8, LANES), jnp.float32)


def mark(token_ref):
    token_ref[...] = jnp.zeros_like(token_ref)


def begin(enc_state, gain, queries, ctx_grad, replicas):
    rows, width = enc_state.shape[1:]
    targets = queries.shape[1]
    piece = width // replicas
    half = replicas // 2

    def kernel(enc_ref, gain_ref, query_ref, grad_ref, *refs):
        out_ref, far_ref, token_ref, held, held_gain, sems, far_sems = refs
        mark(token_ref)
        first = [
            pltpu.make_async_copy(enc_ref.at[0], held, sems.at[0]),
            pltpu.make_async_copy(gain_ref, held_gain, sems.at[1]),
        ]
        for copy in first:
            copy.start()
        index = lax.axis_index("dp")
        copies = []
        for i in range(half):
            columns = pl.ds(pl.multiple_of((index ^ (half + i)) * piece, piece), piece)
            for j, ref in enumerate((query_ref, grad_ref)):
                place = far_ref.at[i, j]
                copy = pltpu.make_async_copy(ref.at[0, :, columns], place, far_sems.at[i, j])
                copy.start()
                copies.append(copy)
        for copy in first:
            copy.wait()
        state = held[...].astype(jnp.float32)
        inverse = lax.rsqrt(jnp.mean(state * state, axis=1, keepdims=True) + epsilon)
        out_ref[...] = (state * inverse * held_gain[...]).astype(jnp.bfloat16)
        for copy in copies:
            copy.wait()

    return call(
        kernel,
        [shape((rows, width)), shape((half, 2, targets, piece)), TOKEN],
        moved=4 * rows * width + 4 * targets * width,
        vmem=VMEM_BEGIN,
        in_specs=[ANY] * 4,
        out_specs=[VMEM] * 3,
        scratch_shapes=[
            pltpu.VMEM((rows, width), jnp.bfloat16),
            pltpu.VMEM((1, width), jnp.float32),
            pltpu.SemaphoreType.DMA((2,)),
            pltpu.SemaphoreType.DMA((half, 2)),
        ],
    )(enc_state, gain, queries, ctx_grad)


def split_heads(queries, ctx_grad, groups, replicas, tokens):
    rows, width = queries.shape[1:]
    piece = width // replicas
    count = sum(len(group) for group in groups)

    def kernel(query_ref, grad_ref, *refs):
        *out_refs, token_ref, sems = refs[len(tokens) :]
        index = lax.axis_index("dp")
        copies = []
        for group, out_ref in zip(groups, out_refs, strict=True):
            for i, k in enumerate(group):
                columns = pl.ds(pl.multiple_of((index ^ k) * piece, piece), piece)
                for j, ref in enumerate((query_ref, grad_ref)):
                    sem = sems.at[len(copies)]
                    copy = pltpu.make_async_copy(ref.at[0, :, columns], out_ref.at[i, j], sem)
                    copy.start()
                    copies.append(copy)
        mark(token_ref)
        for copy in copies:
            copy.wait()

    *shares, token = call(
        kernel,
        [shape((len(group), 2, rows, piece)) for group in groups] + [TOKEN],
        moved=8 * rows * width,
        in_specs=[ANY] * (2 + len(tokens)),
        out_specs=[VMEM] * (len(groups) + 1),
        scratch_shapes=[pltpu.SemaphoreType.DMA((2 * count,))],
    )(queries, ctx_grad, *tokens)
    return shares, token


def add_blocks(blocks, tokens=(), mem_len=None):
    rows, width = blocks[0].shape
    assert rows <= 256
    scalars = [] if mem_len is None else [mem_len]

    def kernel(*refs):
        total = refs[0][...]
        for ref in refs[1 : len(blocks)]:
            total = total + ref[...]
        out_ref = refs[-1]
        out_ref[:, :width] = total
        if scalars:
            columns = jnp.full((rows, LANES), refs[len(blocks)][0].astype(jnp.float32))
            out_ref[:, width:] = columns.astype(jnp.bfloat16)

    return call(
        kernel,
        shape((rows, width + LANES * len(scalars))),
        moved=8 * blocks[0].size,
        in_specs=[VMEM] * len(blocks) + [SMEM] * len(scalars) + [ANY] * len(tokens),
        out_specs=VMEM,
    )(*blocks, *scalars, *tokens)


def stack_rows(first, second, tokens):
    rows, width = first.shape

    def kernel(first_ref, second_ref, *refs):
        out_ref = refs[-1]
        out_ref[:rows] = first_ref[...]
        out_ref[rows:] = second_ref[...]

    return call(
        kernel,
        shape((2 * rows, width)),
        moved=8 * first.size,
        in_specs=[VMEM] * 2 + [ANY] * len(tokens),
        out_specs=VMEM,
    )(first, second, *tokens)


def join_heads(shares):
    replicas, rows, piece = shares.shape

    def kernel(share_ref, out_ref, token_ref, sems):
        copies = []
        for k in range(replicas):
            columns = pl.ds(k * piece, piece)
            copy = pltpu.make_async_copy(share_ref.at[k], out_ref.at[0, :, columns], sems.at[k])
            copy.start()
            copies.append(copy)
        mark(token_ref)
        for copy in copies:
            copy.wait()

    return call(
        kernel,
        [shape((1, rows, replicas * piece)), TOKEN],
        moved=4 * rows * replicas * piece,
        in_specs=[VMEM],
        out_specs=[ANY, VMEM],
        scratch_shapes=[pltpu.SemaphoreType.DMA((replicas,))],
    )(shares)


def hold_weights(w_key, w_value, tokens):
    steps = 4
    step = w_key.shape[1] // steps

    def kernel(wk_ref, wv_ref, *refs):
        *out_refs, token_ref, sems = refs[len(tokens) :]
        copies = []
        for i in range(steps):
            rows = pl.ds(i * step, step)
            for j, (ref, out_ref) in enumerate(zip((wk_ref, wv_ref), out_refs, strict=True)):
                copy = pltpu.make_async_copy(ref.at[0, rows], out_ref.at[0, rows], sems.at[i, j])
                copy.start()
                copies.append(copy)
        mark(token_ref)
        for copy in copies:
            copy.wait()

    *held, token = call(
        kernel,
        [shape(w_key.shape)] * 2 + [TOKEN],
        flops=COST_HOLD,
        moved=4 * w_key.size,
        vmem=36,
        in_specs=[ANY] * (2 + len(tokens)),
        out_specs=[ANY, ANY, VMEM],
        scratch_shapes=[pltpu.SemaphoreType.DMA((steps, 2))],
    )(w_key, w_value, *tokens)
    return held, token


def project(memory, w_key, w_value):
    rows = memory.shape[0]
    depth, width = w_key.shape[1:]

    def kernel(memory_ref, wk_ref, wv_ref, key_ref, value_ref):
        key_ref[...] = dot(memory_ref[:, :depth], wk_ref[0]).astype(jnp.bfloat16)
        value_ref[...] = dot(memory_ref[:, :depth], wv_ref[0]).astype(jnp.bfloat16)

    return call(
        kernel,
        [shape((rows, width))] * 2,
        flops=4 * rows * depth * width,
        moved=4 * depth * width,
        in_specs=[VMEM] * 3,
        out_specs=[VMEM] * 2,
    )(memory, w_key, w_value)


def attend(memory, keys, values, shares, half):
    count = len(shares)
    rows = memory.shape[0] // count
    depth = memory.shape[1] - LANES
    width = keys.shape[1]
    targets = shares[0].shape[2]
    scale = HEAD_DIM ** (-0.5)
    heads = width // HEAD_DIM

    def kernel(memory_ref, key_ref, value_ref, *refs):
        share_refs = refs[:count]
        dk_ref, dv_ref, low_ref, score_ref, grad_ref = refs[count:]
        blocks = []
        for h in range(heads):
            for p in range(count):
                head, own = slice(h * HEAD_DIM, (h + 1) * HEAD_DIM), slice(p * rows, (p + 1) * rows)
                blocks.append((head, own, share_refs[p]))
        for i, (head, own, share_ref) in enumerate(blocks):
            query, grad = share_ref[0, 0, :, head], share_ref[0, 1, :, head]
            score_ref[i] = dot(key_ref[own, head], query, ((1,), (1,)))
            grad_ref[i] = dot(value_ref[own, head], grad, ((1,), (1,)))
        token = lax.broadcasted_iota(jnp.int32, (rows, targets), 0).astype(jnp.float32)
        firsts = [memory_ref[p * rows : p * rows + 1, depth : depth + 1] for p in range(count)]
        valid = jnp.stack([token < first.astype(jnp.float32) for first in firsts])
        for h in range(heads):
            here = slice(h * count, (h + 1) * count)
            scores = jnp.where(valid, score_ref[here] * scale, -1e30)
            exponent = jnp.exp(scores - jnp.max(scores, axis=1, keepdims=True))
            probs = exponent / jnp.sum(exponent, axis=1, keepdims=True)
            grad_probs = grad_ref[here]
            delta = jnp.sum(probs * grad_probs, axis=1, keepdims=True)
            low_ref[0, here] = (probs * (grad_probs - delta) * scale).astype(jnp.bfloat16)
            low_ref[1, here] = probs.astype(jnp.bfloat16)
        is_decoder = (lax.axis_index("section") >= half).astype(jnp.float32)
        for i, (head, own, share_ref) in enumerate(blocks):
            query, grad = share_ref[0, 0, :, head], share_ref[0, 1, :, head]
            dk_ref[own, head] = dot(low_ref[0, i], query).astype(jnp.bfloat16)
            dv_ref[own, head] = (dot(low_ref[1, i], grad) * is_decoder).astype(jnp.bfloat16)

    scores = (heads * count, rows, targets)
    return call(
        kernel,
        [shape((count * rows, width))] * 2 + [shape((2, *scores))],
        flops=8 * count * rows * targets * width,
        moved=8 * count * targets * width,
        in_specs=[VMEM] * (count + 3),
        out_specs=[VMEM] * 3,
        scratch_shapes=[
            *[pltpu.VMEM(scores, jnp.float32)] * 2,
        ],
    )(memory, keys, values, *shares)


def query_grads(scores, keys, order, tokens):
    count = len(order)
    rows = keys.shape[0] // count
    width = keys.shape[1]
    targets = scores.shape[3]

    def kernel(score_ref, key_ref, *refs):
        out_ref, token_ref = refs[-2:]
        mark(token_ref)
        index = lax.axis_index("dp")
        for h in range(width // HEAD_DIM):
            head = slice(h * HEAD_DIM, (h + 1) * HEAD_DIM)
            for p, k in enumerate(order):
                key = key_ref[p * rows : (p + 1) * rows, head]
                grad = dot(score_ref[0, h * count + p], key, ((0,), (0,)))
                out_ref[index ^ k, :, head] = grad.astype(jnp.bfloat16)

    return call(
        kernel,
        [shape((count, targets, width)), TOKEN],
        flops=2 * count * rows * targets * width,
        moved=4 * count * targets * width,
        in_specs=[VMEM] * 2 + [ANY] * len(tokens),
        out_specs=[VMEM] * 2,
    )(scores, keys, *tokens)


def follow(block, tokens):
    def kernel(*refs):
        del refs

    return call(
        kernel,
        shape(block.shape, block.dtype),
        in_specs=[ANY] * (1 + len(tokens)),
        out_specs=ANY,
        input_output_aliases={0: 0},
    )(block, *tokens)


def memory_part(memory, w_key, w_value, dk, dv, gain):
    rows = memory.shape[0]
    depth, width = w_key.shape[1:]
    tile = 512
    steps = depth // tile
    keep = rows // 2

    def kernel(memory_ref, dk_ref, dv_ref, wk_ref, wv_ref, gain_ref, keep_ref, sent_ref, out_ref):
        for f in range(steps):
            here = slice(f * tile, (f + 1) * tile)
            part = dot(wk_ref[0, here, :], dk_ref[...], ((1,), (1,)))
            part = (part + dot(wv_ref[0, here, :], dv_ref[...], ((1,), (1,)))).T
            keep_ref[:, here] = part[:keep]
            sent_ref[:, here] = part[keep:].astype(jnp.bfloat16)
            terms = part * memory_ref[:, here].astype(jnp.float32)
            total = jnp.sum(terms, axis=0, keepdims=True) / gain_ref[:, here]
            for i in range(tile // LANES):
                place = (f * tile) // LANES + i
                out_ref[place : place + 1, :] = total[:, i * LANES : (i + 1) * LANES]
        put_gain(out_ref[...], sent_ref)

    return call(
        kernel,
        [
            shape((keep, depth), jnp.float32),
            shape((keep, depth + 2 * LANES)),
            shape((depth // LANES, LANES), jnp.float32),
        ],
        flops=4 * rows * depth * width,
        moved=4 * depth * width,
        in_specs=[VMEM] * 6,
        out_specs=[VMEM] * 3,
    )(memory, dk, dv, w_key, w_value, gain)


def put_gain(gain, sent_ref):
    rows = gain.shape[0]
    depth = sent_ref.shape[1] - 2 * LANES
    assert sent_ref.shape[0] >= rows
    high = gain.astype(jnp.bfloat16)
    if sent_ref.shape[0] > rows:
        sent_ref[rows:, depth:] = jnp.zeros((sent_ref.shape[0] - rows, 2 * LANES), jnp.bfloat16)
    sent_ref[:rows, depth : depth + LANES] = high
    sent_ref[:rows, depth + LANES :] = (gain - high.astype(jnp.float32)).astype(jnp.bfloat16)


def add_share(kept, came, gain, last, tokens=()):
    rows, depth = kept.shape
    half = rows if last else rows // 2

    def kernel(kept_ref, came_ref, gain_ref, *refs):
        sent_ref, out_ref, *more_refs = refs[len(tokens) :]
        out = gain_ref.shape[0]
        came_gain = came_ref[:out, depth:].astype(jnp.float32)
        total_gain = gain_ref[...] + (came_gain[:, :LANES] + came_gain[:, LANES:])
        out_ref[...] = total_gain
        total = kept_ref[:half] + came_ref[:half, :depth].astype(jnp.float32)
        if last:
            sent_ref[...] = total.astype(jnp.bfloat16)
        else:
            keep_ref, token_ref = more_refs
            keep_ref[...] = total
            other = kept_ref[half:] + came_ref[half:, :depth].astype(jnp.float32)
            sent_ref[:, :depth] = other.astype(jnp.bfloat16)
            put_gain(total_gain, sent_ref)
            mark(token_ref)

    more = [] if last else [shape((half, depth), jnp.float32), TOKEN]
    return call(
        kernel,
        [
            shape((half, depth + (0 if last else 2 * LANES))),
            shape(gain.shape, jnp.float32),
            *more,
        ],
        moved=10 * rows * depth,
        in_specs=[VMEM] * 3 + [ANY] * len(tokens),
        out_specs=[VMEM] * (2 + len(more)),
    )(kept, came, gain, *tokens)


def add_sections(own, came):
    count = len(came)

    def kernel(own_ref, *refs):
        out_ref, token_ref = refs[-2:]
        total = own_ref[...].astype(jnp.float32)
        for ref in refs[:count]:
            total = total + ref[...].astype(jnp.float32)
        out_ref[...] = total.astype(jnp.bfloat16)
        mark(token_ref)

    return call(
        kernel,
        [shape(own.shape), TOKEN],
        flops=COST_SUM,
        moved=6 * own.size,
        in_specs=[VMEM] * (1 + count),
        out_specs=[VMEM] * 2,
    )(own, *came)


def add_gain(own, came, token):
    def kernel(own_ref, came_ref, _, out_ref):
        out_ref[...] = own_ref[...] + came_ref[...]

    return call(
        kernel,
        shape(own.shape, jnp.float32),
        flops=COST_GAIN,
        in_specs=[VMEM] * 2 + [ANY],
        out_specs=VMEM,
    )(own, came, token)


def add_gains(terms, token):
    def kernel(own_ref, other_ref, first_ref, second_ref, _, out_ref):
        out_ref[...] = (own_ref[...] + other_ref[...]) + (first_ref[...] + second_ref[...])

    return call(
        kernel,
        shape(terms[0].shape, jnp.float32),
        in_specs=[VMEM] * 4 + [ANY],
        out_specs=VMEM,
    )(*terms, token)


def weight_grads(memory, width, first, last, dk, dv, before, tokens=()):
    rows = memory.shape[0]
    columns = dk.shape[1]
    tile = TILE

    def kernel(memory_ref, dk_ref, dv_ref, *refs):
        key_ref, value_ref, token_ref = refs[-3:]
        key_ref[0] = dot(memory_ref[...], dk_ref[...], ((0,), (0,))).astype(jnp.bfloat16)
        value_ref[0] = dot(memory_ref[...], dv_ref[...], ((0,), (0,))).astype(jnp.bfloat16)
        mark(token_ref)

    piece = pl.BlockSpec((rows, tile), lambda f: (0, first + f))
    whole = pl.BlockSpec((rows, columns), lambda f: (0, 0))
    out = pl.BlockSpec((1, tile, columns), lambda f: (0, first + f, 0))
    inputs = 3 + len(tokens)
    *grads, token = call(
        kernel,
        [shape((1, width, columns))] * 2 + [TOKEN],
        flops=4 * rows * tile * columns * (last - first),
        moved=4 * tile * columns * (last - first),
        grid=(last - first,),
        in_specs=[piece, whole, whole] + [ANY] * (len(tokens) + len(before)),
        out_specs=[out] * 2 + [pl.BlockSpec(TOKEN.shape, lambda f: (0, 0))],
        vmem=24,
        input_output_aliases={inputs + i: i for i in range(len(before))},
    )(memory, dk, dv, *tokens, *before)
    return grads, token


def finish(holder, enc_state, gain, terms, tokens):
    rows, width = enc_state.shape[1:]

    def kernel(enc_ref, gain_ref, *refs):
        state = enc_ref[0].astype(jnp.float32)
        inverse = lax.rsqrt(jnp.mean(state * state, axis=1, keepdims=True) + epsilon)
        normed = state * inverse
        own = [ref[...].astype(jnp.float32) for ref in refs[: len(terms)]]
        scaled = sum(own[1:], own[0]) * gain_ref[...]
        mean = jnp.mean(scaled * normed, axis=1, keepdims=True)
        grad = inverse * (scaled - normed * mean)
        is_holder = lax.axis_index("section") == holder
        refs[-2][0] = jnp.where(is_holder, grad, 0.0).astype(jnp.bfloat16)
        mark(refs[-1])

    return call(
        kernel,
        [shape((1, rows, width)), TOKEN],
        moved=8 * rows * width,
        in_specs=[VMEM] * (2 + len(terms)) + [ANY] * len(tokens),
        out_specs=[VMEM] * 2,
    )(enc_state, gain, *terms, *tokens)


def on_device(enc_state, final_gain, queries, w_key, w_value, ctx_grad, mem_len):
    sections = lax.axis_size("section")
    replicas = lax.axis_size("dp")
    half = sections // 2
    bits = replicas.bit_length() - 1
    assert replicas == 1 << bits and half & (half - 1) == 0 and half > 1 and bits > 1
    gain = final_gain[None]

    def over_dp(block, k):
        pairs = [
            (s * replicas + d, s * replicas + (d ^ k))
            for s in range(half, sections)
            for d in range(replicas)
        ]
        return lax.ppermute(block, BOTH, pairs)

    def over_section(block, pairs):
        pairs = [(a * replicas + d, b * replicas + d) for a, b in pairs for d in range(replicas)]
        return lax.ppermute(block, BOTH, pairs)

    order = [0]
    for bit in reversed(range(bits)):
        order = order + [k ^ (1 << bit) for k in order]
    rounds = section_rounds(sections)

    memory, far, begun = begin(enc_state, gain, queries, ctx_grad, replicas)
    came_far = over_dp(far, replicas // 2)
    groups = [[k for k in range(1 << bit, 2 << bit)] for bit in reversed(range(bits - 1))]
    came = [over_section(memory, group) for group in split_pairs(rounds[0])]
    arrived = [came[0]]
    weights, held = hold_weights(w_key, w_value, [begun])
    holding = add_blocks(came, [held])
    near, split = split_heads(queries, ctx_grad, [*groups, [0]], replicas, [holding])
    for stage in rounds[1:]:
        arrived += [over_section(holding, group) for group in split_pairs(stage)]
        length = mem_len if stage is rounds[-1] else None
        holding = add_blocks(arrived, [split], length)
    blocks, tokens = {replicas // 2: came_far}, []
    for bit, share in zip(reversed(range(bits - 1)), near, strict=False):
        size = 1 << bit
        passed = {k ^ size: over_dp(b[size : 2 * size], size) for k, b in blocks.items()}
        blocks = blocks | passed | {size: over_dp(share, size)}
        tokens.append(blocks[size])
    blocks[0] = near[-1]
    shares = [blocks[k] for k in order]
    for bit in reversed(range(bits)):
        holding = stack_rows(holding, over_dp(holding, 1 << bit), tokens)
        tokens = []
    pieces = holding
    keys, values = project(pieces, *weights)
    dk, dv, scores = attend(pieces, keys, values, shares, half)

    kept, sent, gain_part = memory_part(pieces, *weights, dk, dv, gain)
    width = enc_state.shape[2]
    decoders = range(half, sections)
    token = None
    for bit in range(bits):
        last = bit == bits - 1
        came = over_dp(sent, 1 << bit)
        tokens = []
        if not bit:
            dq, done = query_grads(scores, keys, order, [gain_part])
            tokens = [done]
        if last:
            grads, done = weight_grads(pieces, width, 0, width // TILE, dk, dv, [], [token])
            tokens = [done]
        sent, gain_part, *more = add_share(kept, came, gain_part, last, tokens)
        if not last:
            kept, token = more
    key_weight_grad, value_weight_grad = grads
    dq = follow(dq, [gain_part])
    for number, stage in reversed(list(enumerate(rounds))):
        came = [over_section(sent, [(b, a) for a, b in group]) for group in split_pairs(stage)]
        if number:
            sent, token = add_sections(sent, came)
    step = 1
    while step < half // 2:
        came_gain = over_section(gain_part, [(s, s ^ step) for s in decoders])
        gain_part = add_gain(gain_part, came_gain, token)
        step *= 2
    places = [(i % step) * 2 + i // step for i in range(half)]
    terms = [
        gain_part,
        over_section(gain_part, [(s, s ^ step) for s in decoders]),
        over_section(gain_part, [(half + i, places[i]) for i in range(half)]),
        over_section(gain_part, [(half + i, places[i ^ step]) for i in range(half)]),
    ]

    query_grad, joined = join_heads(
        lax.all_to_all(dq, "dp", split_axis=0, concat_axis=0, tiled=True)
    )
    state_grad, done = finish(half - 1, enc_state, gain, came, [joined])
    gain_grad = add_gains(terms, done).reshape(width)
    return (query_grad, key_weight_grad, value_weight_grad, state_grad, gain_grad)


def solution(mesh):
    placed = (
        P("section", "dp", None),
        P(),
        P("section", "dp", None),
        P("section", None, "dp"),
        P("section", None, "dp"),
        P("section", "dp", None),
        P("dp"),
    )
    return jax.shard_map(
        on_device,
        mesh=mesh,
        in_specs=placed,
        out_specs=(
            P("section", "dp", None),
            P("section", None, "dp"),
            P("section", None, "dp"),
            P("section", "dp", None),
            P(),
        ),
        check_vma=False,
    )
```

```python
import jax
import jax.numpy as jnp
from jax import lax
from jax.experimental import pallas as pl
from jax.experimental.pallas import tpu as pltpu
from jax.sharding import PartitionSpec as P

HEAD_DIM = 256
epsilon = 1e-06
BOTH = ("section", "dp")
LANES = 128
TILE = 1024
VMEM_BEGIN = 54
COST_HOLD = 1 << 30
COST_SUM = 3 << 30
COST_GAIN = 1 << 32


def section_rounds(sections):
    half = sections // 2
    source = half - 1
    first = min(half + 1, sections - 1)
    held = {source, first}
    rounds = [[(source, first)]]
    if source > 0 and half + 2 < sections:
        rounds[0].append((source, source - 1))
        held.add(source - 1)
    stage = []
    for a, b in ((first, first + 2), (source - 1, source + 3), (first, first - 1)):
        if a in held and half <= b < sections and b not in held:
            stage.append((a, b))
            held.add(b)
    if stage:
        rounds.append(stage)
    while not held.issuperset(range(half, sections)):
        have = [s for s in sorted(held) if s >= half]
        stage = []
        for a in have:
            b = a + len(have)
            if b < sections and b not in held:
                stage.append((a, b))
                held.add(b)
        rounds.append(stage)
    return rounds


def split_pairs(stage):
    groups = []
    for a, b in stage:
        for group in groups:
            if all(a != c and b != e for c, e in group):
                group.append((a, b))
                break
        else:
            groups.append([(a, b)])
    return groups


def call(kernel, out_shape, flops=0, moved=0, vmem=16, **options):
    return pl.pallas_call(
        kernel,
        out_shape=out_shape,
        compiler_params=pltpu.CompilerParams(vmem_limit_bytes=vmem << 20),
        cost_estimate=pl.CostEstimate(flops=flops, bytes_accessed=moved, transcendentals=0),
        **options,
    )


def shape(dims, dtype=jnp.bfloat16):
    return jax.ShapeDtypeStruct(dims, dtype)


def dot(a, b, dims=((1,), (0,))):
    return lax.dot_general(a, b, (dims, ((), ())), preferred_element_type=jnp.float32)


SMEM = pl.BlockSpec(memory_space=pltpu.SMEM)
VMEM = pl.BlockSpec(memory_space=pltpu.VMEM)
ANY = pl.BlockSpec(memory_space=pl.ANY)
TOKEN = shape((8, LANES), jnp.float32)


def mark(token_ref):
    token_ref[...] = jnp.zeros_like(token_ref)


def begin(enc_state, gain, queries, ctx_grad, replicas):
    rows, width = enc_state.shape[1:]
    targets = queries.shape[1]
    piece = width // replicas
    half = replicas // 2

    def kernel(enc_ref, gain_ref, query_ref, grad_ref, *refs):
        out_ref, far_ref, token_ref, held, held_gain, sems, far_sems = refs
        mark(token_ref)
        first = [
            pltpu.make_async_copy(enc_ref.at[0], held, sems.at[0]),
            pltpu.make_async_copy(gain_ref, held_gain, sems.at[1]),
        ]
        for copy in first:
            copy.start()
        index = lax.axis_index("dp")
        copies = []
        for i in range(half):
            columns = pl.ds(pl.multiple_of((index ^ (half + i)) * piece, piece), piece)
            for j, ref in enumerate((query_ref, grad_ref)):
                place = far_ref.at[i, j]
                copy = pltpu.make_async_copy(ref.at[0, :, columns], place, far_sems.at[i, j])
                copy.start()
                copies.append(copy)
        for copy in first:
            copy.wait()
        state = held[...].astype(jnp.float32)
        inverse = lax.rsqrt(jnp.mean(state * state, axis=1, keepdims=True) + epsilon)
        out_ref[...] = (state * inverse * held_gain[...]).astype(jnp.bfloat16)
        for copy in copies:
            copy.wait()

    return call(
        kernel,
        [shape((rows, width)), shape((half, 2, targets, piece)), TOKEN],
        moved=4 * rows * width + 4 * targets * width,
        vmem=VMEM_BEGIN,
        in_specs=[ANY] * 4,
        out_specs=[VMEM] * 3,
        scratch_shapes=[
            pltpu.VMEM((rows, width), jnp.bfloat16),
            pltpu.VMEM((1, width), jnp.float32),
            pltpu.SemaphoreType.DMA((2,)),
            pltpu.SemaphoreType.DMA((half, 2)),
        ],
    )(enc_state, gain, queries, ctx_grad)


def split_heads(queries, ctx_grad, groups, replicas, tokens):
    rows, width = queries.shape[1:]
    piece = width // replicas
    count = sum(len(group) for group in groups)

    def kernel(query_ref, grad_ref, *refs):
        *out_refs, token_ref, sems = refs[len(tokens) :]
        index = lax.axis_index("dp")
        copies = []
        for group, out_ref in zip(groups, out_refs, strict=True):
            for i, k in enumerate(group):
                columns = pl.ds(pl.multiple_of((index ^ k) * piece, piece), piece)
                for j, ref in enumerate((query_ref, grad_ref)):
                    sem = sems.at[len(copies)]
                    copy = pltpu.make_async_copy(ref.at[0, :, columns], out_ref.at[i, j], sem)
                    copy.start()
                    copies.append(copy)
        mark(token_ref)
        for copy in copies:
            copy.wait()

    *shares, token = call(
        kernel,
        [shape((len(group), 2, rows, piece)) for group in groups] + [TOKEN],
        moved=8 * rows * width,
        in_specs=[ANY] * (2 + len(tokens)),
        out_specs=[VMEM] * (len(groups) + 1),
        scratch_shapes=[pltpu.SemaphoreType.DMA((2 * count,))],
    )(queries, ctx_grad, *tokens)
    return shares, token


def add_blocks(blocks, tokens=(), mem_len=None):
    rows, width = blocks[0].shape
    assert rows <= 256
    scalars = [] if mem_len is None else [mem_len]

    def kernel(*refs):
        total = refs[0][...]
        for ref in refs[1 : len(blocks)]:
            total = total + ref[...]
        out_ref = refs[-1]
        out_ref[:, :width] = total
        if scalars:
            columns = jnp.full((rows, LANES), refs[len(blocks)][0].astype(jnp.float32))
            out_ref[:, width:] = columns.astype(jnp.bfloat16)

    return call(
        kernel,
        shape((rows, width + LANES * len(scalars))),
        moved=8 * blocks[0].size,
        in_specs=[VMEM] * len(blocks) + [SMEM] * len(scalars) + [ANY] * len(tokens),
        out_specs=VMEM,
    )(*blocks, *scalars, *tokens)


def stack_rows(first, second, tokens):
    rows, width = first.shape

    def kernel(first_ref, second_ref, *refs):
        out_ref = refs[-1]
        out_ref[:rows] = first_ref[...]
        out_ref[rows:] = second_ref[...]

    return call(
        kernel,
        shape((2 * rows, width)),
        moved=8 * first.size,
        in_specs=[VMEM] * 2 + [ANY] * len(tokens),
        out_specs=VMEM,
    )(first, second, *tokens)


def hold_weights(w_key, w_value, tokens):
    steps = 4
    step = w_key.shape[1] // steps

    def kernel(wk_ref, wv_ref, *refs):
        *out_refs, token_ref, sems = refs[len(tokens) :]
        copies = []
        for i in range(steps):
            rows = pl.ds(i * step, step)
            for j, (ref, out_ref) in enumerate(zip((wk_ref, wv_ref), out_refs, strict=True)):
                copy = pltpu.make_async_copy(ref.at[0, rows], out_ref.at[0, rows], sems.at[i, j])
                copy.start()
                copies.append(copy)
        mark(token_ref)
        for copy in copies:
            copy.wait()

    *held, token = call(
        kernel,
        [shape(w_key.shape)] * 2 + [TOKEN],
        flops=COST_HOLD,
        moved=4 * w_key.size,
        vmem=36,
        in_specs=[ANY] * (2 + len(tokens)),
        out_specs=[ANY, ANY, VMEM],
        scratch_shapes=[pltpu.SemaphoreType.DMA((steps, 2))],
    )(w_key, w_value, *tokens)
    return held, token


def project(memory, w_key, w_value):
    rows = memory.shape[0]
    depth, width = w_key.shape[1:]

    def kernel(memory_ref, wk_ref, wv_ref, key_ref, value_ref):
        key_ref[...] = dot(memory_ref[:, :depth], wk_ref[0]).astype(jnp.bfloat16)
        value_ref[...] = dot(memory_ref[:, :depth], wv_ref[0]).astype(jnp.bfloat16)

    return call(
        kernel,
        [shape((rows, width))] * 2,
        flops=4 * rows * depth * width,
        moved=4 * depth * width,
        in_specs=[VMEM] * 3,
        out_specs=[VMEM] * 2,
    )(memory, w_key, w_value)


def attend(memory, keys, values, shares, half):
    count = len(shares)
    rows = memory.shape[0] // count
    depth = memory.shape[1] - LANES
    width = keys.shape[1]
    targets = shares[0].shape[2]
    scale = HEAD_DIM ** (-0.5)
    heads = width // HEAD_DIM

    def kernel(memory_ref, key_ref, value_ref, *refs):
        share_refs = refs[:count]
        dk_ref, dv_ref, low_ref, score_ref, grad_ref = refs[count:]
        blocks = []
        for h in range(heads):
            for p in range(count):
                head, own = slice(h * HEAD_DIM, (h + 1) * HEAD_DIM), slice(p * rows, (p + 1) * rows)
                blocks.append((head, own, share_refs[p]))
        for i, (head, own, share_ref) in enumerate(blocks):
            query, grad = share_ref[0, 0, :, head], share_ref[0, 1, :, head]
            score_ref[i] = dot(key_ref[own, head], query, ((1,), (1,)))
            grad_ref[i] = dot(value_ref[own, head], grad, ((1,), (1,)))
        token = lax.broadcasted_iota(jnp.int32, (rows, targets), 0).astype(jnp.float32)
        firsts = [memory_ref[p * rows : p * rows + 1, depth : depth + 1] for p in range(count)]
        valid = jnp.stack([token < first.astype(jnp.float32) for first in firsts])
        for h in range(heads):
            here = slice(h * count, (h + 1) * count)
            scores = jnp.where(valid, score_ref[here] * scale, -1e30)
            exponent = jnp.exp(scores - jnp.max(scores, axis=1, keepdims=True))
            probs = exponent / jnp.sum(exponent, axis=1, keepdims=True)
            grad_probs = grad_ref[here]
            delta = jnp.sum(probs * grad_probs, axis=1, keepdims=True)
            low_ref[0, here] = (probs * (grad_probs - delta) * scale).astype(jnp.bfloat16)
            low_ref[1, here] = probs.astype(jnp.bfloat16)
        is_decoder = (lax.axis_index("section") >= half).astype(jnp.float32)
        for i, (head, own, share_ref) in enumerate(blocks):
            query, grad = share_ref[0, 0, :, head], share_ref[0, 1, :, head]
            dk_ref[own, head] = dot(low_ref[0, i], query).astype(jnp.bfloat16)
            dv_ref[own, head] = (dot(low_ref[1, i], grad) * is_decoder).astype(jnp.bfloat16)

    scores = (heads * count, rows, targets)
    return call(
        kernel,
        [shape((count * rows, width))] * 2 + [shape((2, *scores))],
        flops=8 * count * rows * targets * width,
        moved=8 * count * targets * width,
        in_specs=[VMEM] * (count + 3),
        out_specs=[VMEM] * 3,
        scratch_shapes=[
            *[pltpu.VMEM(scores, jnp.float32)] * 2,
        ],
    )(memory, keys, values, *shares)


def query_grads(scores, keys, order, tokens):
    count = len(order)
    rows = keys.shape[0] // count
    width = keys.shape[1]
    targets = scores.shape[3]

    def kernel(score_ref, key_ref, *refs):
        out_ref, token_ref = refs[-2:]
        mark(token_ref)
        index = lax.axis_index("dp")
        for h in range(width // HEAD_DIM):
            head = slice(h * HEAD_DIM, (h + 1) * HEAD_DIM)
            for p, k in enumerate(order):
                key = key_ref[p * rows : (p + 1) * rows, head]
                grad = dot(score_ref[0, h * count + p], key, ((0,), (0,)))
                out_ref[index ^ k, :, head] = grad.astype(jnp.bfloat16)

    return call(
        kernel,
        [shape((count, targets, width)), TOKEN],
        flops=2 * count * rows * targets * width,
        moved=4 * count * targets * width,
        in_specs=[VMEM] * 2 + [ANY] * len(tokens),
        out_specs=[VMEM] * 2,
    )(scores, keys, *tokens)


def follow(block, tokens):
    def kernel(*refs):
        del refs

    return call(
        kernel,
        shape(block.shape, block.dtype),
        in_specs=[ANY] * (1 + len(tokens)),
        out_specs=ANY,
        input_output_aliases={0: 0},
    )(block, *tokens)


def memory_part(memory, w_key, w_value, dk, dv, gain):
    rows = memory.shape[0]
    depth, width = w_key.shape[1:]
    tile = 512
    steps = depth // tile
    keep = rows // 2

    def kernel(memory_ref, dk_ref, dv_ref, wk_ref, wv_ref, gain_ref, keep_ref, sent_ref, out_ref):
        for f in range(steps):
            here = slice(f * tile, (f + 1) * tile)
            part = dot(wk_ref[0, here, :], dk_ref[...], ((1,), (1,)))
            part = (part + dot(wv_ref[0, here, :], dv_ref[...], ((1,), (1,)))).T
            keep_ref[:, here] = part[:keep]
            sent_ref[:, here] = part[keep:].astype(jnp.bfloat16)
            terms = part * memory_ref[:, here].astype(jnp.float32)
            total = jnp.sum(terms, axis=0, keepdims=True) / gain_ref[:, here]
            for i in range(tile // LANES):
                place = (f * tile) // LANES + i
                out_ref[place : place + 1, :] = total[:, i * LANES : (i + 1) * LANES]
        put_gain(out_ref[...], sent_ref)

    return call(
        kernel,
        [
            shape((keep, depth), jnp.float32),
            shape((keep, depth + 2 * LANES)),
            shape((depth // LANES, LANES), jnp.float32),
        ],
        flops=4 * rows * depth * width,
        moved=4 * depth * width,
        in_specs=[VMEM] * 6,
        out_specs=[VMEM] * 3,
    )(memory, dk, dv, w_key, w_value, gain)


def put_gain(gain, sent_ref):
    rows = gain.shape[0]
    depth = sent_ref.shape[1] - 2 * LANES
    assert sent_ref.shape[0] >= rows
    high = gain.astype(jnp.bfloat16)
    if sent_ref.shape[0] > rows:
        sent_ref[rows:, depth:] = jnp.zeros((sent_ref.shape[0] - rows, 2 * LANES), jnp.bfloat16)
    sent_ref[:rows, depth : depth + LANES] = high
    sent_ref[:rows, depth + LANES :] = (gain - high.astype(jnp.float32)).astype(jnp.bfloat16)


def add_share(kept, came, gain, last, tokens=()):
    rows, depth = kept.shape
    half = rows if last else rows // 2

    def kernel(kept_ref, came_ref, gain_ref, *refs):
        sent_ref, out_ref, *more_refs = refs[len(tokens) :]
        out = gain_ref.shape[0]
        came_gain = came_ref[:out, depth:].astype(jnp.float32)
        total_gain = gain_ref[...] + (came_gain[:, :LANES] + came_gain[:, LANES:])
        out_ref[...] = total_gain
        total = kept_ref[:half] + came_ref[:half, :depth].astype(jnp.float32)
        if last:
            sent_ref[...] = total.astype(jnp.bfloat16)
        else:
            keep_ref, token_ref = more_refs
            keep_ref[...] = total
            other = kept_ref[half:] + came_ref[half:, :depth].astype(jnp.float32)
            sent_ref[:, :depth] = other.astype(jnp.bfloat16)
            put_gain(total_gain, sent_ref)
            mark(token_ref)

    more = [] if last else [shape((half, depth), jnp.float32), TOKEN]
    return call(
        kernel,
        [
            shape((half, depth + (0 if last else 2 * LANES))),
            shape(gain.shape, jnp.float32),
            *more,
        ],
        moved=10 * rows * depth,
        in_specs=[VMEM] * 3 + [ANY] * len(tokens),
        out_specs=[VMEM] * (2 + len(more)),
    )(kept, came, gain, *tokens)


def add_sections(own, came):
    count = len(came)

    def kernel(own_ref, *refs):
        out_ref, token_ref = refs[-2:]
        total = own_ref[...].astype(jnp.float32)
        for ref in refs[:count]:
            total = total + ref[...].astype(jnp.float32)
        out_ref[...] = total.astype(jnp.bfloat16)
        mark(token_ref)

    return call(
        kernel,
        [shape(own.shape), TOKEN],
        flops=COST_SUM,
        moved=6 * own.size,
        in_specs=[VMEM] * (1 + count),
        out_specs=[VMEM] * 2,
    )(own, *came)


def add_gain(own, came, token):
    def kernel(own_ref, came_ref, _, out_ref):
        out_ref[...] = own_ref[...] + came_ref[...]

    return call(
        kernel,
        shape(own.shape, jnp.float32),
        flops=COST_GAIN,
        in_specs=[VMEM] * 2 + [ANY],
        out_specs=VMEM,
    )(own, came, token)


def close(terms, shares, tokens):
    replicas, rows, piece = shares.shape

    def kernel(own_ref, other_ref, first_ref, second_ref, share_ref, *refs):
        out_ref, query_ref, held, sems = refs[len(tokens) :]
        held[...] = (own_ref[...] + other_ref[...]) + (first_ref[...] + second_ref[...])
        copies = [pltpu.make_async_copy(held, out_ref, sems.at[replicas])]
        for k in range(replicas):
            columns = pl.ds(k * piece, piece)
            place = query_ref.at[0, :, columns]
            copies.append(pltpu.make_async_copy(share_ref.at[k], place, sems.at[k]))
        for copy in copies:
            copy.start()
        for copy in copies:
            copy.wait()

    return call(
        kernel,
        [shape(terms[0].shape, jnp.float32), shape((1, rows, replicas * piece))],
        moved=4 * shares.size,
        in_specs=[VMEM] * 5 + [ANY] * len(tokens),
        out_specs=[ANY, ANY],
        scratch_shapes=[
            pltpu.VMEM(terms[0].shape, jnp.float32),
            pltpu.SemaphoreType.DMA((replicas + 1,)),
        ],
    )(*terms, shares, *tokens)


def weight_grads(memory, width, first, last, dk, dv, before, tokens=()):
    rows = memory.shape[0]
    columns = dk.shape[1]
    tile = TILE

    def kernel(memory_ref, dk_ref, dv_ref, *refs):
        key_ref, value_ref, token_ref = refs[-3:]
        key_ref[0] = dot(memory_ref[...], dk_ref[...], ((0,), (0,))).astype(jnp.bfloat16)
        value_ref[0] = dot(memory_ref[...], dv_ref[...], ((0,), (0,))).astype(jnp.bfloat16)
        mark(token_ref)

    piece = pl.BlockSpec((rows, tile), lambda f: (0, first + f))
    whole = pl.BlockSpec((rows, columns), lambda f: (0, 0))
    out = pl.BlockSpec((1, tile, columns), lambda f: (0, first + f, 0))
    inputs = 3 + len(tokens)
    *grads, token = call(
        kernel,
        [shape((1, width, columns))] * 2 + [TOKEN],
        flops=4 * rows * tile * columns * (last - first),
        moved=4 * tile * columns * (last - first),
        grid=(last - first,),
        in_specs=[piece, whole, whole] + [ANY] * (len(tokens) + len(before)),
        out_specs=[out] * 2 + [pl.BlockSpec(TOKEN.shape, lambda f: (0, 0))],
        vmem=24,
        input_output_aliases={inputs + i: i for i in range(len(before))},
    )(memory, dk, dv, *tokens, *before)
    return grads, token


def finish(holder, enc_state, gain, terms):
    rows, width = enc_state.shape[1:]

    def kernel(enc_ref, gain_ref, *refs):
        state = enc_ref[0].astype(jnp.float32)
        inverse = lax.rsqrt(jnp.mean(state * state, axis=1, keepdims=True) + epsilon)
        normed = state * inverse
        own = [ref[...].astype(jnp.float32) for ref in refs[: len(terms)]]
        scaled = sum(own[1:], own[0]) * gain_ref[...]
        mean = jnp.mean(scaled * normed, axis=1, keepdims=True)
        grad = inverse * (scaled - normed * mean)
        is_holder = lax.axis_index("section") == holder
        refs[-2][0] = jnp.where(is_holder, grad, 0.0).astype(jnp.bfloat16)
        mark(refs[-1])

    return call(
        kernel,
        [shape((1, rows, width)), TOKEN],
        moved=8 * rows * width,
        in_specs=[VMEM] * (2 + len(terms)),
        out_specs=[VMEM] * 2,
    )(enc_state, gain, *terms)


def on_device(enc_state, final_gain, queries, w_key, w_value, ctx_grad, mem_len):
    sections = lax.axis_size("section")
    replicas = lax.axis_size("dp")
    half = sections // 2
    bits = replicas.bit_length() - 1
    assert replicas == 1 << bits and half & (half - 1) == 0 and half > 1 and bits > 1
    gain = final_gain[None]

    def over_dp(block, k):
        pairs = [
            (s * replicas + d, s * replicas + (d ^ k))
            for s in range(half, sections)
            for d in range(replicas)
        ]
        return lax.ppermute(block, BOTH, pairs)

    def over_section(block, pairs):
        pairs = [(a * replicas + d, b * replicas + d) for a, b in pairs for d in range(replicas)]
        return lax.ppermute(block, BOTH, pairs)

    order = [0]
    for bit in reversed(range(bits)):
        order = order + [k ^ (1 << bit) for k in order]
    rounds = section_rounds(sections)

    memory, far, begun = begin(enc_state, gain, queries, ctx_grad, replicas)
    came_far = over_dp(far, replicas // 2)
    groups = [[k for k in range(1 << bit, 2 << bit)] for bit in reversed(range(bits - 1))]
    came = [over_section(memory, group) for group in split_pairs(rounds[0])]
    arrived = [came[0]]
    weights, held = hold_weights(w_key, w_value, [begun])
    holding = add_blocks(came, [held])
    near, split = split_heads(queries, ctx_grad, [*groups, [0]], replicas, [holding])
    for stage in rounds[1:]:
        arrived += [over_section(holding, group) for group in reversed(split_pairs(stage))]
        length = mem_len if stage is rounds[-1] else None
        holding = add_blocks(arrived, [split], length)
    blocks, tokens = {replicas // 2: came_far}, []
    for bit, share in zip(reversed(range(bits - 1)), near, strict=False):
        size = 1 << bit
        passed = {k ^ size: over_dp(b[size : 2 * size], size) for k, b in blocks.items()}
        blocks = blocks | passed | {size: over_dp(share, size)}
        tokens.append(blocks[size])
    blocks[0] = near[-1]
    shares = [blocks[k] for k in order]
    for bit in reversed(range(bits)):
        holding = stack_rows(holding, over_dp(holding, 1 << bit), tokens)
        tokens = []
    pieces = holding
    keys, values = project(pieces, *weights)
    dk, dv, scores = attend(pieces, keys, values, shares, half)

    kept, sent, gain_part = memory_part(pieces, *weights, dk, dv, gain)
    width = enc_state.shape[2]
    decoders = range(half, sections)
    token = None
    for bit in range(bits):
        last = bit == bits - 1
        came = over_dp(sent, 1 << bit)
        tokens = []
        if not bit:
            dq, done = query_grads(scores, keys, order, [gain_part])
            tokens = [done]
        if last:
            grads, done = weight_grads(pieces, width, 0, width // TILE, dk, dv, [], [token])
            tokens = [done]
        sent, gain_part, *more = add_share(kept, came, gain_part, last, tokens)
        if not last:
            kept, token = more
    key_weight_grad, value_weight_grad = grads
    dq = follow(dq, [gain_part])
    for number, stage in reversed(list(enumerate(rounds))):
        groups = reversed(split_pairs(stage))
        came = [over_section(sent, [(b, a) for a, b in group]) for group in groups]
        if number:
            sent, token = add_sections(sent, came)
    step = 1
    while step < half // 2:
        came_gain = over_section(gain_part, [(s, s ^ step) for s in decoders])
        gain_part = add_gain(gain_part, came_gain, token)
        step *= 2
    places = [(i % step) * 2 + i // step for i in range(half)]
    terms = [
        gain_part,
        over_section(gain_part, [(s, s ^ step) for s in decoders]),
        over_section(gain_part, [(half + i, places[i]) for i in range(half)]),
        over_section(gain_part, [(half + i, places[i ^ step]) for i in range(half)]),
    ]

    state_grad, done = finish(half - 1, enc_state, gain, came)
    dq = lax.all_to_all(dq, "dp", split_axis=0, concat_axis=0, tiled=True)
    gain_grad, query_grad = close(terms, dq, [done])
    gain_grad = gain_grad.reshape(final_gain.shape)
    return (query_grad, key_weight_grad, value_weight_grad, state_grad, gain_grad)


def solution(mesh):
    placed = (
        P("section", "dp", None),
        P(),
        P("section", "dp", None),
        P("section", None, "dp"),
        P("section", None, "dp"),
        P("section", "dp", None),
        P("dp"),
    )
    return jax.shard_map(
        on_device,
        mesh=mesh,
        in_specs=placed,
        out_specs=(
            P("section", "dp", None),
            P("section", None, "dp"),
            P("section", None, "dp"),
            P("section", "dp", None),
            P(),
        ),
        check_vma=False,
    )
```

```python
import jax
import jax.numpy as jnp
from jax import lax
from jax.experimental import pallas as pl
from jax.experimental.pallas import tpu as pltpu
from jax.sharding import PartitionSpec as P

HEAD_DIM = 256
epsilon = 1e-06
BOTH = ("section", "dp")
LANES = 128
TILE = 1024
VMEM_BEGIN = 54
COST_HOLD = 1 << 30
COST_SUM = 3 << 30
COST_GAIN = 1 << 32


def section_rounds(sections):
    half = sections // 2
    source = half - 1
    first = min(half + 1, sections - 1)
    held = {source, first}
    rounds = [[(source, first)]]
    if source > 0 and half + 2 < sections:
        rounds[0].append((source, source - 1))
        held.add(source - 1)
    stage = []
    for a, b in ((first, first + 2), (source - 1, source + 3), (first, first - 1)):
        if a in held and half <= b < sections and b not in held:
            stage.append((a, b))
            held.add(b)
    if stage:
        rounds.append(stage)
    while not held.issuperset(range(half, sections)):
        have = [s for s in sorted(held) if s >= half]
        stage = []
        for a in have:
            b = a + len(have)
            if b < sections and b not in held:
                stage.append((a, b))
                held.add(b)
        rounds.append(stage)
    return rounds


def split_pairs(stage):
    groups = []
    for a, b in stage:
        for group in groups:
            if all(a != c and b != e for c, e in group):
                group.append((a, b))
                break
        else:
            groups.append([(a, b)])
    return groups


def call(kernel, out_shape, flops=0, moved=0, vmem=16, **options):
    return pl.pallas_call(
        kernel,
        out_shape=out_shape,
        compiler_params=pltpu.CompilerParams(vmem_limit_bytes=vmem << 20),
        cost_estimate=pl.CostEstimate(flops=flops, bytes_accessed=moved, transcendentals=0),
        **options,
    )


def shape(dims, dtype=jnp.bfloat16):
    return jax.ShapeDtypeStruct(dims, dtype)


def dot(a, b, dims=((1,), (0,))):
    return lax.dot_general(a, b, (dims, ((), ())), preferred_element_type=jnp.float32)


SMEM = pl.BlockSpec(memory_space=pltpu.SMEM)
VMEM = pl.BlockSpec(memory_space=pltpu.VMEM)
ANY = pl.BlockSpec(memory_space=pl.ANY)
TOKEN = shape((8, LANES), jnp.float32)


def mark(token_ref):
    token_ref[...] = jnp.zeros_like(token_ref)


def begin(enc_state, gain, queries, ctx_grad, replicas):
    rows, width = enc_state.shape[1:]
    targets = queries.shape[1]
    piece = width // replicas
    half = replicas // 2

    def kernel(enc_ref, gain_ref, query_ref, grad_ref, *refs):
        out_ref, far_ref, token_ref, held, held_gain, sems, far_sems = refs
        mark(token_ref)
        first = [
            pltpu.make_async_copy(enc_ref.at[0], held, sems.at[0]),
            pltpu.make_async_copy(gain_ref, held_gain, sems.at[1]),
        ]
        for copy in first:
            copy.start()
        index = lax.axis_index("dp")
        copies = []
        for i in range(half):
            columns = pl.ds(pl.multiple_of((index ^ (half + i)) * piece, piece), piece)
            for j, ref in enumerate((query_ref, grad_ref)):
                place = far_ref.at[i, j]
                copy = pltpu.make_async_copy(ref.at[0, :, columns], place, far_sems.at[i, j])
                copy.start()
                copies.append(copy)
        for copy in first:
            copy.wait()
        state = held[...].astype(jnp.float32)
        inverse = lax.rsqrt(jnp.mean(state * state, axis=1, keepdims=True) + epsilon)
        out_ref[...] = (state * inverse * held_gain[...]).astype(jnp.bfloat16)
        for copy in copies:
            copy.wait()

    return call(
        kernel,
        [shape((rows, width)), shape((half, 2, targets, piece)), TOKEN],
        moved=4 * rows * width + 4 * targets * width,
        vmem=VMEM_BEGIN,
        in_specs=[ANY] * 4,
        out_specs=[VMEM] * 3,
        scratch_shapes=[
            pltpu.VMEM((rows, width), jnp.bfloat16),
            pltpu.VMEM((1, width), jnp.float32),
            pltpu.SemaphoreType.DMA((2,)),
            pltpu.SemaphoreType.DMA((half, 2)),
        ],
    )(enc_state, gain, queries, ctx_grad)


def split_heads(queries, ctx_grad, groups, replicas, tokens):
    rows, width = queries.shape[1:]
    piece = width // replicas
    count = sum(len(group) for group in groups)

    def kernel(query_ref, grad_ref, *refs):
        *out_refs, token_ref, sems = refs[len(tokens) :]
        index = lax.axis_index("dp")
        copies = []
        for group, out_ref in zip(groups, out_refs, strict=True):
            for i, k in enumerate(group):
                columns = pl.ds(pl.multiple_of((index ^ k) * piece, piece), piece)
                for j, ref in enumerate((query_ref, grad_ref)):
                    sem = sems.at[len(copies)]
                    copy = pltpu.make_async_copy(ref.at[0, :, columns], out_ref.at[i, j], sem)
                    copy.start()
                    copies.append(copy)
        mark(token_ref)
        for copy in copies:
            copy.wait()

    *shares, token = call(
        kernel,
        [shape((len(group), 2, rows, piece)) for group in groups] + [TOKEN],
        moved=8 * rows * width,
        in_specs=[ANY] * (2 + len(tokens)),
        out_specs=[VMEM] * (len(groups) + 1),
        scratch_shapes=[pltpu.SemaphoreType.DMA((2 * count,))],
    )(queries, ctx_grad, *tokens)
    return shares, token


def add_blocks(blocks, tokens=(), mem_len=None):
    rows, width = blocks[0].shape
    assert rows <= 256
    scalars = [] if mem_len is None else [mem_len]

    def kernel(*refs):
        total = refs[0][...]
        for ref in refs[1 : len(blocks)]:
            total = total + ref[...]
        out_ref = refs[-1]
        out_ref[:, :width] = total
        if scalars:
            columns = jnp.full((rows, LANES), refs[len(blocks)][0].astype(jnp.float32))
            out_ref[:, width:] = columns.astype(jnp.bfloat16)

    return call(
        kernel,
        shape((rows, width + LANES * len(scalars))),
        moved=8 * blocks[0].size,
        in_specs=[VMEM] * len(blocks) + [SMEM] * len(scalars) + [ANY] * len(tokens),
        out_specs=VMEM,
    )(*blocks, *scalars, *tokens)


def stack_rows(blocks, places, tokens):
    rows, width = blocks[0].shape
    count = len(blocks)

    def kernel(*refs):
        for i, ref in zip(places, refs[len(tokens) :], strict=False):
            refs[-1][i * rows : (i + 1) * rows] = ref[...]

    return call(
        kernel,
        shape((count * rows, width)),
        moved=4 * count * rows * width,
        in_specs=[ANY] * len(tokens) + [VMEM] * count,
        out_specs=VMEM,
    )(*tokens, *blocks)


def hold_weights(w_key, w_value, tokens):
    steps = 4
    step = w_key.shape[1] // steps

    def kernel(wk_ref, wv_ref, *refs):
        *out_refs, token_ref, sems = refs[len(tokens) :]
        copies = []
        for i in range(steps):
            rows = pl.ds(i * step, step)
            for j, (ref, out_ref) in enumerate(zip((wk_ref, wv_ref), out_refs, strict=True)):
                copy = pltpu.make_async_copy(ref.at[0, rows], out_ref.at[0, rows], sems.at[i, j])
                copy.start()
                copies.append(copy)
        mark(token_ref)
        for copy in copies:
            copy.wait()

    *held, token = call(
        kernel,
        [shape(w_key.shape)] * 2 + [TOKEN],
        flops=COST_HOLD,
        moved=4 * w_key.size,
        vmem=36,
        in_specs=[ANY] * (2 + len(tokens)),
        out_specs=[ANY, ANY, VMEM],
        scratch_shapes=[pltpu.SemaphoreType.DMA((steps, 2))],
    )(w_key, w_value, *tokens)
    return held, token


def project(memory, w_key, w_value):
    rows = memory.shape[0]
    depth, width = w_key.shape[1:]

    def kernel(memory_ref, wk_ref, wv_ref, key_ref, value_ref):
        key_ref[...] = dot(memory_ref[:, :depth], wk_ref[0]).astype(jnp.bfloat16)
        value_ref[...] = dot(memory_ref[:, :depth], wv_ref[0]).astype(jnp.bfloat16)

    return call(
        kernel,
        [shape((rows, width))] * 2,
        flops=4 * rows * depth * width,
        moved=4 * depth * width,
        in_specs=[VMEM] * 3,
        out_specs=[VMEM] * 2,
    )(memory, w_key, w_value)


def attend(memory, keys, values, shares, half):
    count = len(shares)
    rows = memory.shape[0] // count
    depth = memory.shape[1] - LANES
    width = keys.shape[1]
    targets = shares[0].shape[2]
    scale = HEAD_DIM ** (-0.5)
    heads = width // HEAD_DIM

    def kernel(memory_ref, key_ref, value_ref, *refs):
        share_refs = refs[:count]
        dk_ref, dv_ref, low_ref, score_ref, grad_ref = refs[count:]
        blocks = []
        for h in range(heads):
            for p in range(count):
                head, own = slice(h * HEAD_DIM, (h + 1) * HEAD_DIM), slice(p * rows, (p + 1) * rows)
                blocks.append((head, own, share_refs[p]))
        for i, (head, own, share_ref) in enumerate(blocks):
            query, grad = share_ref[0, 0, :, head], share_ref[0, 1, :, head]
            score_ref[i] = dot(key_ref[own, head], query, ((1,), (1,)))
            grad_ref[i] = dot(value_ref[own, head], grad, ((1,), (1,)))
        token = lax.broadcasted_iota(jnp.int32, (rows, targets), 0).astype(jnp.float32)
        firsts = [memory_ref[p * rows : p * rows + 1, depth : depth + 1] for p in range(count)]
        valid = jnp.stack([token < first.astype(jnp.float32) for first in firsts])
        for h in range(heads):
            here = slice(h * count, (h + 1) * count)
            scores = jnp.where(valid, score_ref[here] * scale, -1e30)
            exponent = jnp.exp(scores - jnp.max(scores, axis=1, keepdims=True))
            probs = exponent / jnp.sum(exponent, axis=1, keepdims=True)
            grad_probs = grad_ref[here]
            delta = jnp.sum(probs * grad_probs, axis=1, keepdims=True)
            low_ref[0, here] = (probs * (grad_probs - delta) * scale).astype(jnp.bfloat16)
            low_ref[1, here] = probs.astype(jnp.bfloat16)
        is_decoder = (lax.axis_index("section") >= half).astype(jnp.float32)
        for i, (head, own, share_ref) in enumerate(blocks):
            query, grad = share_ref[0, 0, :, head], share_ref[0, 1, :, head]
            dk_ref[own, head] = dot(low_ref[0, i], query).astype(jnp.bfloat16)
            dv_ref[own, head] = (dot(low_ref[1, i], grad) * is_decoder).astype(jnp.bfloat16)

    scores = (heads * count, rows, targets)
    return call(
        kernel,
        [shape((count * rows, width))] * 2 + [shape((2, *scores))],
        flops=8 * count * rows * targets * width,
        moved=8 * count * targets * width,
        in_specs=[VMEM] * (count + 3),
        out_specs=[VMEM] * 3,
        scratch_shapes=[
            *[pltpu.VMEM(scores, jnp.float32)] * 2,
        ],
    )(memory, keys, values, *shares)


def query_grads(scores, keys, order, tokens):
    count = len(order)
    rows = keys.shape[0] // count
    width = keys.shape[1]
    targets = scores.shape[3]

    def kernel(score_ref, key_ref, *refs):
        out_ref, token_ref = refs[-2:]
        mark(token_ref)
        index = lax.axis_index("dp")
        for h in range(width // HEAD_DIM):
            head = slice(h * HEAD_DIM, (h + 1) * HEAD_DIM)
            for p, k in enumerate(order):
                key = key_ref[p * rows : (p + 1) * rows, head]
                grad = dot(score_ref[0, h * count + p], key, ((0,), (0,)))
                out_ref[index ^ k, :, head] = grad.astype(jnp.bfloat16)

    return call(
        kernel,
        [shape((count, targets, width)), TOKEN],
        flops=2 * count * rows * targets * width,
        moved=4 * count * targets * width,
        in_specs=[VMEM] * 2 + [ANY] * len(tokens),
        out_specs=[VMEM] * 2,
    )(scores, keys, *tokens)


def follow(block, tokens):
    def kernel(*refs):
        del refs

    return call(
        kernel,
        shape(block.shape, block.dtype),
        in_specs=[ANY] * (1 + len(tokens)),
        out_specs=ANY,
        input_output_aliases={0: 0},
    )(block, *tokens)


def memory_part(memory, w_key, w_value, dk, dv, gain):
    rows = memory.shape[0]
    depth, width = w_key.shape[1:]
    tile = 512
    steps = depth // tile
    keep = rows // 2

    def kernel(memory_ref, dk_ref, dv_ref, wk_ref, wv_ref, gain_ref, keep_ref, sent_ref, out_ref):
        for f in range(steps):
            here = slice(f * tile, (f + 1) * tile)
            part = dot(wk_ref[0, here, :], dk_ref[...], ((1,), (1,)))
            part = (part + dot(wv_ref[0, here, :], dv_ref[...], ((1,), (1,)))).T
            keep_ref[:, here] = part[:keep]
            sent_ref[:, here] = part[keep:].astype(jnp.bfloat16)
            terms = part * memory_ref[:, here].astype(jnp.float32)
            total = jnp.sum(terms, axis=0, keepdims=True) / gain_ref[:, here]
            for i in range(tile // LANES):
                place = (f * tile) // LANES + i
                out_ref[place : place + 1, :] = total[:, i * LANES : (i + 1) * LANES]
        put_gain(out_ref[...], sent_ref)

    return call(
        kernel,
        [
            shape((keep, depth), jnp.float32),
            shape((keep, depth + 2 * LANES)),
            shape((depth // LANES, LANES), jnp.float32),
        ],
        flops=4 * rows * depth * width,
        moved=4 * depth * width,
        in_specs=[VMEM] * 6,
        out_specs=[VMEM] * 3,
    )(memory, dk, dv, w_key, w_value, gain)


def put_gain(gain, sent_ref):
    rows = gain.shape[0]
    depth = sent_ref.shape[1] - 2 * LANES
    assert sent_ref.shape[0] >= rows
    high = gain.astype(jnp.bfloat16)
    if sent_ref.shape[0] > rows:
        sent_ref[rows:, depth:] = jnp.zeros((sent_ref.shape[0] - rows, 2 * LANES), jnp.bfloat16)
    sent_ref[:rows, depth : depth + LANES] = high
    sent_ref[:rows, depth + LANES :] = (gain - high.astype(jnp.float32)).astype(jnp.bfloat16)


def add_share(kept, came, gain, last, tokens=()):
    rows, depth = kept.shape
    half = rows if last else rows // 2

    def kernel(kept_ref, came_ref, gain_ref, *refs):
        sent_ref, out_ref, *more_refs = refs[len(tokens) :]
        out = gain_ref.shape[0]
        came_gain = came_ref[:out, depth:].astype(jnp.float32)
        total_gain = gain_ref[...] + (came_gain[:, :LANES] + came_gain[:, LANES:])
        out_ref[...] = total_gain
        total = kept_ref[:half] + came_ref[:half, :depth].astype(jnp.float32)
        if last:
            sent_ref[...] = total.astype(jnp.bfloat16)
        else:
            keep_ref, token_ref = more_refs
            keep_ref[...] = total
            other = kept_ref[half:] + came_ref[half:, :depth].astype(jnp.float32)
            sent_ref[:, :depth] = other.astype(jnp.bfloat16)
            put_gain(total_gain, sent_ref)
            mark(token_ref)

    more = [] if last else [shape((half, depth), jnp.float32), TOKEN]
    return call(
        kernel,
        [
            shape((half, depth + (0 if last else 2 * LANES))),
            shape(gain.shape, jnp.float32),
            *more,
        ],
        moved=10 * rows * depth,
        in_specs=[VMEM] * 3 + [ANY] * len(tokens),
        out_specs=[VMEM] * (2 + len(more)),
    )(kept, came, gain, *tokens)


def add_sections(own, came):
    count = len(came)

    def kernel(own_ref, *refs):
        out_ref, token_ref = refs[-2:]
        total = own_ref[...].astype(jnp.float32)
        for ref in refs[:count]:
            total = total + ref[...].astype(jnp.float32)
        out_ref[...] = total.astype(jnp.bfloat16)
        mark(token_ref)

    return call(
        kernel,
        [shape(own.shape), TOKEN],
        flops=COST_SUM,
        moved=6 * own.size,
        in_specs=[VMEM] * (1 + count),
        out_specs=[VMEM] * 2,
    )(own, *came)


def add_gain(own, came, token):
    def kernel(own_ref, came_ref, _, out_ref):
        out_ref[...] = own_ref[...] + came_ref[...]

    return call(
        kernel,
        shape(own.shape, jnp.float32),
        flops=COST_GAIN,
        in_specs=[VMEM] * 2 + [ANY],
        out_specs=VMEM,
    )(own, came, token)


def close(terms, shares, tokens):
    replicas, rows, piece = shares.shape

    def kernel(own_ref, other_ref, first_ref, second_ref, share_ref, *refs):
        out_ref, query_ref, held, sems = refs[len(tokens) :]
        held[...] = (own_ref[...] + other_ref[...]) + (first_ref[...] + second_ref[...])
        copies = [pltpu.make_async_copy(held, out_ref, sems.at[replicas])]
        for k in range(replicas):
            columns = pl.ds(k * piece, piece)
            place = query_ref.at[0, :, columns]
            copies.append(pltpu.make_async_copy(share_ref.at[k], place, sems.at[k]))
        for copy in copies:
            copy.start()
        for copy in copies:
            copy.wait()

    return call(
        kernel,
        [shape(terms[0].shape, jnp.float32), shape((1, rows, replicas * piece))],
        moved=4 * shares.size,
        in_specs=[VMEM] * 5 + [ANY] * len(tokens),
        out_specs=[ANY, ANY],
        scratch_shapes=[
            pltpu.VMEM(terms[0].shape, jnp.float32),
            pltpu.SemaphoreType.DMA((replicas + 1,)),
        ],
    )(*terms, shares, *tokens)


def weight_grads(memory, width, first, last, dk, dv, before, tokens=()):
    rows = memory.shape[0]
    columns = dk.shape[1]
    tile = TILE

    def kernel(memory_ref, dk_ref, dv_ref, *refs):
        key_ref, value_ref, token_ref = refs[-3:]
        key_ref[0] = dot(memory_ref[...], dk_ref[...], ((0,), (0,))).astype(jnp.bfloat16)
        value_ref[0] = dot(memory_ref[...], dv_ref[...], ((0,), (0,))).astype(jnp.bfloat16)
        mark(token_ref)

    piece = pl.BlockSpec((rows, tile), lambda f: (0, first + f))
    whole = pl.BlockSpec((rows, columns), lambda f: (0, 0))
    out = pl.BlockSpec((1, tile, columns), lambda f: (0, first + f, 0))
    inputs = 3 + len(tokens)
    *grads, token = call(
        kernel,
        [shape((1, width, columns))] * 2 + [TOKEN],
        flops=4 * rows * tile * columns * (last - first),
        moved=4 * tile * columns * (last - first),
        grid=(last - first,),
        in_specs=[piece, whole, whole] + [ANY] * (len(tokens) + len(before)),
        out_specs=[out] * 2 + [pl.BlockSpec(TOKEN.shape, lambda f: (0, 0))],
        vmem=24,
        input_output_aliases={inputs + i: i for i in range(len(before))},
    )(memory, dk, dv, *tokens, *before)
    return grads, token


def finish(holder, enc_state, gain, terms):
    rows, width = enc_state.shape[1:]

    def kernel(enc_ref, gain_ref, *refs):
        state = enc_ref[0].astype(jnp.float32)
        inverse = lax.rsqrt(jnp.mean(state * state, axis=1, keepdims=True) + epsilon)
        normed = state * inverse
        own = [ref[...].astype(jnp.float32) for ref in refs[: len(terms)]]
        scaled = sum(own[1:], own[0]) * gain_ref[...]
        mean = jnp.mean(scaled * normed, axis=1, keepdims=True)
        grad = inverse * (scaled - normed * mean)
        is_holder = lax.axis_index("section") == holder
        refs[-2][0] = jnp.where(is_holder, grad, 0.0).astype(jnp.bfloat16)
        mark(refs[-1])

    return call(
        kernel,
        [shape((1, rows, width)), TOKEN],
        moved=8 * rows * width,
        in_specs=[VMEM] * (2 + len(terms)),
        out_specs=[VMEM] * 2,
    )(enc_state, gain, *terms)


def on_device(enc_state, final_gain, queries, w_key, w_value, ctx_grad, mem_len):
    sections = lax.axis_size("section")
    replicas = lax.axis_size("dp")
    half = sections // 2
    bits = replicas.bit_length() - 1
    assert replicas == 1 << bits and half & (half - 1) == 0 and half > 1 and bits > 1
    gain = final_gain[None]

    def over_dp(block, k):
        pairs = [
            (s * replicas + d, s * replicas + (d ^ k))
            for s in range(half, sections)
            for d in range(replicas)
        ]
        return lax.ppermute(block, BOTH, pairs)

    def over_section(block, pairs):
        pairs = [(a * replicas + d, b * replicas + d) for a, b in pairs for d in range(replicas)]
        return lax.ppermute(block, BOTH, pairs)

    order = [0]
    for bit in reversed(range(bits)):
        order = order + [k ^ (1 << bit) for k in order]
    rounds = section_rounds(sections)

    memory, far, begun = begin(enc_state, gain, queries, ctx_grad, replicas)
    came_far = over_dp(far, replicas // 2)
    groups = [[k for k in range(1 << bit, 2 << bit)] for bit in reversed(range(bits - 1))]
    came = [over_section(memory, group) for group in split_pairs(rounds[0])]
    arrived = [came[0]]
    weights, held = hold_weights(w_key, w_value, [begun])
    holding = add_blocks(came, [held])
    near, split = split_heads(queries, ctx_grad, [*groups, [0]], replicas, [holding])
    for stage in rounds[1:]:
        arrived += [over_section(holding, group) for group in reversed(split_pairs(stage))]
        length = mem_len if stage is rounds[-1] else None
        holding = add_blocks(arrived, [split], length)
    blocks = {replicas // 2: came_far}
    for bit, share in zip(reversed(range(bits - 1)), near, strict=False):
        size = 1 << bit
        passed = {k ^ size: over_dp(b[size : 2 * size], size) for k, b in blocks.items()}
        blocks = blocks | passed | {size: over_dp(share, size)}
    pieces = {0: holding}
    for k in range(1, replicas):
        step = k & -k
        block = pieces[k ^ step]
        if k ^ step:
            block = stack_rows([block], [0], [pieces[step], blocks[step]])
        pieces[k] = over_dp(block, step)
    places = [order.index(k) for k in range(replicas)]
    passed = [blocks[k] for k in range(1, replicas)]
    pieces = stack_rows([pieces[k] for k in range(replicas)], places, passed)
    blocks[0] = near[-1]
    shares = [blocks[k] for k in order]
    keys, values = project(pieces, *weights)
    dk, dv, scores = attend(pieces, keys, values, shares, half)

    kept, sent, gain_part = memory_part(pieces, *weights, dk, dv, gain)
    width = enc_state.shape[2]
    decoders = range(half, sections)
    token = None
    for bit in range(bits):
        last = bit == bits - 1
        came = over_dp(sent, 1 << bit)
        tokens = []
        if not bit:
            dq, done = query_grads(scores, keys, order, [gain_part])
            tokens = [done]
        if last:
            grads, done = weight_grads(pieces, width, 0, width // TILE, dk, dv, [], [token])
            tokens = [done]
        sent, gain_part, *more = add_share(kept, came, gain_part, last, tokens)
        if not last:
            kept, token = more
    key_weight_grad, value_weight_grad = grads
    dq = follow(dq, [gain_part])
    for number, stage in reversed(list(enumerate(rounds))):
        groups = reversed(split_pairs(stage))
        came = [over_section(sent, [(b, a) for a, b in group]) for group in groups]
        if number:
            sent, token = add_sections(sent, came)
    step = 1
    while step < half // 2:
        came_gain = over_section(gain_part, [(s, s ^ step) for s in decoders])
        gain_part = add_gain(gain_part, came_gain, token)
        step *= 2
    places = [(i % step) * 2 + i // step for i in range(half)]
    terms = [
        gain_part,
        over_section(gain_part, [(s, s ^ step) for s in decoders]),
        over_section(gain_part, [(half + i, places[i]) for i in range(half)]),
        over_section(gain_part, [(half + i, places[i ^ step]) for i in range(half)]),
    ]

    state_grad, done = finish(half - 1, enc_state, gain, came)
    dq = lax.all_to_all(dq, "dp", split_axis=0, concat_axis=0, tiled=True)
    gain_grad, query_grad = close(terms, dq, [done])
    gain_grad = gain_grad.reshape(final_gain.shape)
    return (query_grad, key_weight_grad, value_weight_grad, state_grad, gain_grad)


def solution(mesh):
    placed = (
        P("section", "dp", None),
        P(),
        P("section", "dp", None),
        P("section", None, "dp"),
        P("section", None, "dp"),
        P("section", "dp", None),
        P("dp"),
    )
    return jax.shard_map(
        on_device,
        mesh=mesh,
        in_specs=placed,
        out_specs=(
            P("section", "dp", None),
            P("section", None, "dp"),
            P("section", None, "dp"),
            P("section", "dp", None),
            P(),
        ),
        check_vma=False,
    )
```

```python
import jax
import jax.numpy as jnp
from jax import lax
from jax.experimental import pallas as pl
from jax.experimental.pallas import tpu as pltpu
from jax.sharding import PartitionSpec as P

HEAD_DIM = 256
epsilon = 1e-06
BOTH = ("section", "dp")
LANES = 128
TILE = 1024
VMEM_BEGIN = 54
COST_HOLD = 1 << 30
COST_SUM = 3 << 30
COST_GAIN = 1 << 32


def section_rounds(sections):
    half = sections // 2
    source = half - 1
    first = min(half + 1, sections - 1)
    held = {source, first}
    rounds = [[(source, first)]]
    if source > 0 and half + 2 < sections:
        rounds[0].append((source, source - 1))
        held.add(source - 1)
    stage = []
    for a, b in ((first, first + 2), (source - 1, source + 3), (first, first - 1)):
        if a in held and half <= b < sections and b not in held:
            stage.append((a, b))
            held.add(b)
    if stage:
        rounds.append(stage)
    while not held.issuperset(range(half, sections)):
        have = [s for s in sorted(held) if s >= half]
        stage = []
        for a in have:
            b = a + len(have)
            if b < sections and b not in held:
                stage.append((a, b))
                held.add(b)
        rounds.append(stage)
    return rounds


def split_pairs(stage):
    groups = []
    for a, b in stage:
        for group in groups:
            if all(a != c and b != e for c, e in group):
                group.append((a, b))
                break
        else:
            groups.append([(a, b)])
    return groups


def call(kernel, out_shape, flops=0, moved=0, vmem=16, **options):
    return pl.pallas_call(
        kernel,
        out_shape=out_shape,
        compiler_params=pltpu.CompilerParams(vmem_limit_bytes=vmem << 20),
        cost_estimate=pl.CostEstimate(flops=flops, bytes_accessed=moved, transcendentals=0),
        **options,
    )


def shape(dims, dtype=jnp.bfloat16):
    return jax.ShapeDtypeStruct(dims, dtype)


def dot(a, b, dims=((1,), (0,))):
    return lax.dot_general(a, b, (dims, ((), ())), preferred_element_type=jnp.float32)


SMEM = pl.BlockSpec(memory_space=pltpu.SMEM)
VMEM = pl.BlockSpec(memory_space=pltpu.VMEM)
ANY = pl.BlockSpec(memory_space=pl.ANY)
TOKEN = shape((8, LANES), jnp.float32)


def mark(token_ref):
    token_ref[...] = jnp.zeros_like(token_ref)


def begin(enc_state, gain, queries, ctx_grad, replicas):
    rows, width = enc_state.shape[1:]
    targets = queries.shape[1]
    piece = width // replicas
    half = replicas // 2

    def kernel(enc_ref, gain_ref, query_ref, grad_ref, *refs):
        out_ref, far_ref, token_ref, held, held_gain, sems, far_sems = refs
        mark(token_ref)
        first = [
            pltpu.make_async_copy(enc_ref.at[0], held, sems.at[0]),
            pltpu.make_async_copy(gain_ref, held_gain, sems.at[1]),
        ]
        for copy in first:
            copy.start()
        index = lax.axis_index("dp")
        copies = []
        for i in range(half):
            columns = pl.ds(pl.multiple_of((index ^ (half + i)) * piece, piece), piece)
            for j, ref in enumerate((query_ref, grad_ref)):
                place = far_ref.at[i, j]
                copy = pltpu.make_async_copy(ref.at[0, :, columns], place, far_sems.at[i, j])
                copy.start()
                copies.append(copy)
        for copy in first:
            copy.wait()
        state = held[...].astype(jnp.float32)
        inverse = lax.rsqrt(jnp.mean(state * state, axis=1, keepdims=True) + epsilon)
        out_ref[...] = (state * inverse * held_gain[...]).astype(jnp.bfloat16)
        for copy in copies:
            copy.wait()

    return call(
        kernel,
        [shape((rows, width)), shape((half, 2, targets, piece)), TOKEN],
        moved=4 * rows * width + 4 * targets * width,
        vmem=VMEM_BEGIN,
        in_specs=[ANY] * 4,
        out_specs=[VMEM] * 3,
        scratch_shapes=[
            pltpu.VMEM((rows, width), jnp.bfloat16),
            pltpu.VMEM((1, width), jnp.float32),
            pltpu.SemaphoreType.DMA((2,)),
            pltpu.SemaphoreType.DMA((half, 2)),
        ],
    )(enc_state, gain, queries, ctx_grad)


def split_heads(queries, ctx_grad, groups, replicas, tokens):
    rows, width = queries.shape[1:]
    piece = width // replicas
    count = sum(len(group) for group in groups)

    def kernel(query_ref, grad_ref, *refs):
        *out_refs, token_ref, sems = refs[len(tokens) :]
        index = lax.axis_index("dp")
        copies = []
        for group, out_ref in zip(groups, out_refs, strict=True):
            for i, k in enumerate(group):
                columns = pl.ds(pl.multiple_of((index ^ k) * piece, piece), piece)
                for j, ref in enumerate((query_ref, grad_ref)):
                    sem = sems.at[len(copies)]
                    copy = pltpu.make_async_copy(ref.at[0, :, columns], out_ref.at[i, j], sem)
                    copy.start()
                    copies.append(copy)
        mark(token_ref)
        for copy in copies:
            copy.wait()

    *shares, token = call(
        kernel,
        [shape((len(group), 2, rows, piece)) for group in groups] + [TOKEN],
        moved=8 * rows * width,
        in_specs=[ANY] * (2 + len(tokens)),
        out_specs=[VMEM] * (len(groups) + 1),
        scratch_shapes=[pltpu.SemaphoreType.DMA((2 * count,))],
    )(queries, ctx_grad, *tokens)
    return shares, token


def add_blocks(blocks, tokens=(), mem_len=None):
    rows, width = blocks[0].shape
    assert rows <= 256
    scalars = [] if mem_len is None else [mem_len]

    def kernel(*refs):
        total = refs[0][...]
        for ref in refs[1 : len(blocks)]:
            total = total + ref[...]
        out_ref = refs[-1]
        out_ref[:, :width] = total
        if scalars:
            columns = jnp.full((rows, LANES), refs[len(blocks)][0].astype(jnp.float32))
            out_ref[:, width:] = columns.astype(jnp.bfloat16)

    return call(
        kernel,
        shape((rows, width + LANES * len(scalars))),
        moved=8 * blocks[0].size,
        in_specs=[VMEM] * len(blocks) + [SMEM] * len(scalars) + [ANY] * len(tokens),
        out_specs=VMEM,
    )(*blocks, *scalars, *tokens)


def stack_rows(blocks, places, tokens):
    rows, width = blocks[0].shape
    count = len(blocks)

    def kernel(*refs):
        for i, ref in zip(places, refs[len(tokens) :], strict=False):
            refs[-1][i * rows : (i + 1) * rows] = ref[...]

    return call(
        kernel,
        shape((count * rows, width)),
        moved=4 * count * rows * width,
        in_specs=[ANY] * len(tokens) + [VMEM] * count,
        out_specs=VMEM,
    )(*tokens, *blocks)


def hold_weights(w_key, w_value, tokens):
    steps = 4
    step = w_key.shape[1] // steps

    def kernel(wk_ref, wv_ref, *refs):
        *out_refs, token_ref, sems = refs[len(tokens) :]
        copies = []
        for i in range(steps):
            rows = pl.ds(i * step, step)
            for j, (ref, out_ref) in enumerate(zip((wk_ref, wv_ref), out_refs, strict=True)):
                copy = pltpu.make_async_copy(ref.at[0, rows], out_ref.at[0, rows], sems.at[i, j])
                copy.start()
                copies.append(copy)
        mark(token_ref)
        for copy in copies:
            copy.wait()

    *held, token = call(
        kernel,
        [shape(w_key.shape)] * 2 + [TOKEN],
        flops=COST_HOLD,
        moved=4 * w_key.size,
        vmem=36,
        in_specs=[ANY] * (2 + len(tokens)),
        out_specs=[ANY, ANY, VMEM],
        scratch_shapes=[pltpu.SemaphoreType.DMA((steps, 2))],
    )(w_key, w_value, *tokens)
    return held, token


def project(memory, w_key, w_value):
    rows = memory.shape[0]
    depth, width = w_key.shape[1:]

    def kernel(memory_ref, wk_ref, wv_ref, key_ref, value_ref):
        key_ref[...] = dot(memory_ref[:, :depth], wk_ref[0]).astype(jnp.bfloat16)
        value_ref[...] = dot(memory_ref[:, :depth], wv_ref[0]).astype(jnp.bfloat16)

    return call(
        kernel,
        [shape((rows, width))] * 2,
        flops=4 * rows * depth * width,
        moved=4 * depth * width,
        in_specs=[VMEM] * 3,
        out_specs=[VMEM] * 2,
    )(memory, w_key, w_value)


def attend(memory, keys, values, shares, half):
    count = len(shares)
    rows = memory.shape[0] // count
    depth = memory.shape[1] - LANES
    width = keys.shape[1]
    targets = shares[0].shape[2]
    scale = HEAD_DIM ** (-0.5)
    heads = width // HEAD_DIM

    def kernel(memory_ref, key_ref, value_ref, *refs):
        share_refs = refs[:count]
        dk_ref, dv_ref, low_ref, score_ref, grad_ref = refs[count:]
        blocks = []
        for h in range(heads):
            for p in range(count):
                head, own = slice(h * HEAD_DIM, (h + 1) * HEAD_DIM), slice(p * rows, (p + 1) * rows)
                blocks.append((head, own, share_refs[p]))
        for i, (head, own, share_ref) in enumerate(blocks):
            query, grad = share_ref[0, 0, :, head], share_ref[0, 1, :, head]
            score_ref[i] = dot(key_ref[own, head], query, ((1,), (1,)))
            grad_ref[i] = dot(value_ref[own, head], grad, ((1,), (1,)))
        token = lax.broadcasted_iota(jnp.int32, (rows, targets), 0).astype(jnp.float32)
        firsts = [memory_ref[p * rows : p * rows + 1, depth : depth + 1] for p in range(count)]
        valid = jnp.stack([token < first.astype(jnp.float32) for first in firsts])
        for h in range(heads):
            here = slice(h * count, (h + 1) * count)
            scores = jnp.where(valid, score_ref[here] * scale, -1e30)
            exponent = jnp.exp(scores - jnp.max(scores, axis=1, keepdims=True))
            probs = exponent / jnp.sum(exponent, axis=1, keepdims=True)
            grad_probs = grad_ref[here]
            delta = jnp.sum(probs * grad_probs, axis=1, keepdims=True)
            low_ref[0, here] = (probs * (grad_probs - delta) * scale).astype(jnp.bfloat16)
            low_ref[1, here] = probs.astype(jnp.bfloat16)
        is_decoder = (lax.axis_index("section") >= half).astype(jnp.float32)
        for i, (head, own, share_ref) in enumerate(blocks):
            query, grad = share_ref[0, 0, :, head], share_ref[0, 1, :, head]
            dk_ref[own, head] = dot(low_ref[0, i], query).astype(jnp.bfloat16)
            dv_ref[own, head] = (dot(low_ref[1, i], grad) * is_decoder).astype(jnp.bfloat16)

    scores = (heads * count, rows, targets)
    return call(
        kernel,
        [shape((count * rows, width))] * 2 + [shape((2, *scores))],
        flops=8 * count * rows * targets * width,
        moved=8 * count * targets * width,
        in_specs=[VMEM] * (count + 3),
        out_specs=[VMEM] * 3,
        scratch_shapes=[
            *[pltpu.VMEM(scores, jnp.float32)] * 2,
        ],
    )(memory, keys, values, *shares)


def query_grads(scores, keys, order, tokens):
    count = len(order)
    rows = keys.shape[0] // count
    width = keys.shape[1]
    targets = scores.shape[3]

    def kernel(score_ref, key_ref, *refs):
        out_ref, token_ref = refs[-2:]
        mark(token_ref)
        index = lax.axis_index("dp")
        for h in range(width // HEAD_DIM):
            head = slice(h * HEAD_DIM, (h + 1) * HEAD_DIM)
            for p, k in enumerate(order):
                key = key_ref[p * rows : (p + 1) * rows, head]
                grad = dot(score_ref[0, h * count + p], key, ((0,), (0,)))
                out_ref[index ^ k, :, head] = grad.astype(jnp.bfloat16)

    return call(
        kernel,
        [shape((count, targets, width)), TOKEN],
        flops=2 * count * rows * targets * width,
        moved=4 * count * targets * width,
        in_specs=[VMEM] * 2 + [ANY] * len(tokens),
        out_specs=[VMEM] * 2,
    )(scores, keys, *tokens)


def follow(block, tokens):
    def kernel(*refs):
        del refs

    return call(
        kernel,
        shape(block.shape, block.dtype),
        in_specs=[ANY] * (1 + len(tokens)),
        out_specs=ANY,
        input_output_aliases={0: 0},
    )(block, *tokens)


def memory_part(memory, w_key, w_value, dk, dv, gain):
    rows = memory.shape[0]
    depth, width = w_key.shape[1:]
    tile = 512
    steps = depth // tile
    keep = rows // 2

    def kernel(memory_ref, dk_ref, dv_ref, wk_ref, wv_ref, gain_ref, keep_ref, sent_ref, out_ref):
        for f in range(steps):
            here = slice(f * tile, (f + 1) * tile)
            part = dot(wk_ref[0, here, :], dk_ref[...], ((1,), (1,)))
            part = (part + dot(wv_ref[0, here, :], dv_ref[...], ((1,), (1,)))).T
            keep_ref[:, here] = part[:keep]
            sent_ref[:, here] = part[keep:].astype(jnp.bfloat16)
            terms = part * memory_ref[:, here].astype(jnp.float32)
            total = jnp.sum(terms, axis=0, keepdims=True) / gain_ref[:, here]
            for i in range(tile // LANES):
                place = (f * tile) // LANES + i
                out_ref[place : place + 1, :] = total[:, i * LANES : (i + 1) * LANES]
        put_gain(out_ref[...], sent_ref)

    return call(
        kernel,
        [
            shape((keep, depth), jnp.float32),
            shape((keep, depth + 2 * LANES)),
            shape((depth // LANES, LANES), jnp.float32),
        ],
        flops=4 * rows * depth * width,
        moved=4 * depth * width,
        in_specs=[VMEM] * 6,
        out_specs=[VMEM] * 3,
    )(memory, dk, dv, w_key, w_value, gain)


def put_gain(gain, sent_ref):
    rows = gain.shape[0]
    depth = sent_ref.shape[1] - 2 * LANES
    assert sent_ref.shape[0] >= rows
    high = gain.astype(jnp.bfloat16)
    if sent_ref.shape[0] > rows:
        sent_ref[rows:, depth:] = jnp.zeros((sent_ref.shape[0] - rows, 2 * LANES), jnp.bfloat16)
    sent_ref[:rows, depth : depth + LANES] = high
    sent_ref[:rows, depth + LANES :] = (gain - high.astype(jnp.float32)).astype(jnp.bfloat16)


def add_share(kept, came, gain, last, tokens=()):
    rows, depth = kept.shape
    half = rows if last else rows // 2

    def kernel(kept_ref, came_ref, gain_ref, *refs):
        sent_ref, out_ref, *more_refs = refs[len(tokens) :]
        out = gain_ref.shape[0]
        came_gain = came_ref[:out, depth:].astype(jnp.float32)
        total_gain = gain_ref[...] + (came_gain[:, :LANES] + came_gain[:, LANES:])
        out_ref[...] = total_gain
        total = kept_ref[:half] + came_ref[:half, :depth].astype(jnp.float32)
        if last:
            sent_ref[...] = total.astype(jnp.bfloat16)
        else:
            keep_ref, token_ref = more_refs
            keep_ref[...] = total
            other = kept_ref[half:] + came_ref[half:, :depth].astype(jnp.float32)
            sent_ref[:, :depth] = other.astype(jnp.bfloat16)
            put_gain(total_gain, sent_ref)
            mark(token_ref)

    more = [] if last else [shape((half, depth), jnp.float32), TOKEN]
    return call(
        kernel,
        [
            shape((half, depth + (0 if last else 2 * LANES))),
            shape(gain.shape, jnp.float32),
            *more,
        ],
        moved=10 * rows * depth,
        in_specs=[VMEM] * 3 + [ANY] * len(tokens),
        out_specs=[VMEM] * (2 + len(more)),
    )(kept, came, gain, *tokens)


def add_sections(own, came):
    count = len(came)

    def kernel(own_ref, *refs):
        out_ref, token_ref = refs[-2:]
        total = own_ref[...].astype(jnp.float32)
        for ref in refs[:count]:
            total = total + ref[...].astype(jnp.float32)
        out_ref[...] = total.astype(jnp.bfloat16)
        mark(token_ref)

    return call(
        kernel,
        [shape(own.shape), TOKEN],
        flops=COST_SUM,
        moved=6 * own.size,
        in_specs=[VMEM] * (1 + count),
        out_specs=[VMEM] * 2,
    )(own, *came)


def add_gain(own, came, token):
    def kernel(own_ref, came_ref, _, out_ref):
        out_ref[...] = own_ref[...] + came_ref[...]

    return call(
        kernel,
        shape(own.shape, jnp.float32),
        flops=COST_GAIN,
        in_specs=[VMEM] * 2 + [ANY],
        out_specs=VMEM,
    )(own, came, token)


def close(terms, shares, tokens):
    replicas, rows, piece = shares.shape

    def kernel(own_ref, other_ref, first_ref, second_ref, share_ref, *refs):
        out_ref, query_ref, held, sems = refs[len(tokens) :]
        held[...] = (own_ref[...] + other_ref[...]) + (first_ref[...] + second_ref[...])
        copies = [pltpu.make_async_copy(held, out_ref, sems.at[replicas])]
        for k in range(replicas):
            columns = pl.ds(k * piece, piece)
            place = query_ref.at[0, :, columns]
            copies.append(pltpu.make_async_copy(share_ref.at[k], place, sems.at[k]))
        for copy in copies:
            copy.start()
        for copy in copies:
            copy.wait()

    return call(
        kernel,
        [shape(terms[0].shape, jnp.float32), shape((1, rows, replicas * piece))],
        moved=4 * shares.size,
        in_specs=[VMEM] * 5 + [ANY] * len(tokens),
        out_specs=[ANY, ANY],
        scratch_shapes=[
            pltpu.VMEM(terms[0].shape, jnp.float32),
            pltpu.SemaphoreType.DMA((replicas + 1,)),
        ],
    )(*terms, shares, *tokens)


def weight_grads(memory, width, first, last, dk, dv, before, tokens=()):
    rows = memory.shape[0]
    columns = dk.shape[1]
    tile = TILE

    def kernel(memory_ref, dk_ref, dv_ref, *refs):
        key_ref, value_ref, token_ref = refs[-3:]
        key_ref[0] = dot(memory_ref[...], dk_ref[...], ((0,), (0,))).astype(jnp.bfloat16)
        value_ref[0] = dot(memory_ref[...], dv_ref[...], ((0,), (0,))).astype(jnp.bfloat16)
        mark(token_ref)

    piece = pl.BlockSpec((rows, tile), lambda f: (0, first + f))
    whole = pl.BlockSpec((rows, columns), lambda f: (0, 0))
    out = pl.BlockSpec((1, tile, columns), lambda f: (0, first + f, 0))
    inputs = 3 + len(tokens)
    *grads, token = call(
        kernel,
        [shape((1, width, columns))] * 2 + [TOKEN],
        flops=4 * rows * tile * columns * (last - first),
        moved=4 * tile * columns * (last - first),
        grid=(last - first,),
        in_specs=[piece, whole, whole] + [ANY] * (len(tokens) + len(before)),
        out_specs=[out] * 2 + [pl.BlockSpec(TOKEN.shape, lambda f: (0, 0))],
        vmem=24,
        input_output_aliases={inputs + i: i for i in range(len(before))},
    )(memory, dk, dv, *tokens, *before)
    return grads, token


def finish(holder, enc_state, gain, terms):
    rows, width = enc_state.shape[1:]

    def kernel(enc_ref, gain_ref, *refs):
        state = enc_ref[0].astype(jnp.float32)
        inverse = lax.rsqrt(jnp.mean(state * state, axis=1, keepdims=True) + epsilon)
        normed = state * inverse
        own = [ref[...].astype(jnp.float32) for ref in refs[: len(terms)]]
        scaled = sum(own[1:], own[0]) * gain_ref[...]
        mean = jnp.mean(scaled * normed, axis=1, keepdims=True)
        grad = inverse * (scaled - normed * mean)
        is_holder = lax.axis_index("section") == holder
        refs[-2][0] = jnp.where(is_holder, grad, 0.0).astype(jnp.bfloat16)
        mark(refs[-1])

    return call(
        kernel,
        [shape((1, rows, width)), TOKEN],
        moved=8 * rows * width,
        in_specs=[VMEM] * (2 + len(terms)),
        out_specs=[VMEM] * 2,
    )(enc_state, gain, *terms)


def on_device(enc_state, final_gain, queries, w_key, w_value, ctx_grad, mem_len):
    sections = lax.axis_size("section")
    replicas = lax.axis_size("dp")
    half = sections // 2
    bits = replicas.bit_length() - 1
    assert replicas == 1 << bits and half & (half - 1) == 0 and half > 1 and bits > 1
    gain = final_gain[None]

    def over_dp(block, k):
        pairs = [
            (s * replicas + d, s * replicas + (d ^ k))
            for s in range(half, sections)
            for d in range(replicas)
        ]
        return lax.ppermute(block, BOTH, pairs)

    def over_section(block, pairs):
        pairs = [(a * replicas + d, b * replicas + d) for a, b in pairs for d in range(replicas)]
        return lax.ppermute(block, BOTH, pairs)

    order = [0]
    for bit in reversed(range(bits)):
        order = order + [k ^ (1 << bit) for k in order]
    rounds = section_rounds(sections)

    memory, far, begun = begin(enc_state, gain, queries, ctx_grad, replicas)
    came_far = over_dp(far, replicas // 2)
    groups = [[k for k in range(1 << bit, 2 << bit)] for bit in reversed(range(bits - 1))]
    came = [over_section(memory, group) for group in reversed(split_pairs(rounds[0]))]
    arrived = [came[-1]]
    weights, held = hold_weights(w_key, w_value, [begun])
    holding = add_blocks(came, [held])
    near, split = split_heads(queries, ctx_grad, [*groups, [0]], replicas, [holding])
    for stage in rounds[1:]:
        arrived += [over_section(holding, group) for group in reversed(split_pairs(stage))]
        length = mem_len if stage is rounds[-1] else None
        holding = add_blocks(arrived, [split], length)
    blocks = {replicas // 2: came_far}
    for bit, share in zip(reversed(range(bits - 1)), near, strict=False):
        size = 1 << bit
        passed = {k ^ size: over_dp(b[size : 2 * size], size) for k, b in blocks.items()}
        blocks = blocks | passed | {size: over_dp(share, size)}
    pieces = {0: holding}
    for k in range(1, replicas):
        step = k & -k
        block = pieces[k ^ step]
        if k ^ step:
            block = stack_rows([block], [0], [pieces[step], blocks[step]])
        pieces[k] = over_dp(block, step)
    places = [order.index(k) for k in range(replicas)]
    passed = [blocks[k] for k in range(1, replicas)]
    pieces = stack_rows([pieces[k] for k in range(replicas)], places, passed)
    blocks[0] = near[-1]
    shares = [blocks[k] for k in order]
    keys, values = project(pieces, *weights)
    dk, dv, scores = attend(pieces, keys, values, shares, half)

    kept, sent, gain_part = memory_part(pieces, *weights, dk, dv, gain)
    width = enc_state.shape[2]
    decoders = range(half, sections)
    token = None
    for bit in range(bits):
        last = bit == bits - 1
        came = over_dp(sent, 1 << bit)
        tokens = []
        if not bit:
            dq, done = query_grads(scores, keys, order, [gain_part])
            tokens = [done]
        if last:
            grads, done = weight_grads(pieces, width, 0, width // TILE, dk, dv, [], [token])
            tokens = [done]
        sent, gain_part, *more = add_share(kept, came, gain_part, last, tokens)
        if not last:
            kept, token = more
    key_weight_grad, value_weight_grad = grads
    dq = follow(dq, [gain_part])
    for number, stage in reversed(list(enumerate(rounds))):
        groups = reversed(split_pairs(stage))
        came = [over_section(sent, [(b, a) for a, b in group]) for group in groups]
        if number:
            sent, token = add_sections(sent, came)
    step = 1
    while step < half // 2:
        came_gain = over_section(gain_part, [(s, s ^ step) for s in decoders])
        gain_part = add_gain(gain_part, came_gain, token)
        step *= 2
    places = [(i % step) * 2 + i // step for i in range(half)]
    terms = [
        gain_part,
        over_section(gain_part, [(s, s ^ step) for s in decoders]),
        over_section(gain_part, [(half + i, places[i]) for i in range(half)]),
        over_section(gain_part, [(half + i, places[i ^ step]) for i in range(half)]),
    ]

    state_grad, done = finish(half - 1, enc_state, gain, came)
    dq = lax.all_to_all(dq, "dp", split_axis=0, concat_axis=0, tiled=True)
    gain_grad, query_grad = close(terms, dq, [done])
    gain_grad = gain_grad.reshape(final_gain.shape)
    return (query_grad, key_weight_grad, value_weight_grad, state_grad, gain_grad)


def solution(mesh):
    placed = (
        P("section", "dp", None),
        P(),
        P("section", "dp", None),
        P("section", None, "dp"),
        P("section", None, "dp"),
        P("section", "dp", None),
        P("dp"),
    )
    return jax.shard_map(
        on_device,
        mesh=mesh,
        in_specs=placed,
        out_specs=(
            P("section", "dp", None),
            P("section", None, "dp"),
            P("section", None, "dp"),
            P("section", "dp", None),
            P(),
        ),
        check_vma=False,
    )
```
